32 devices in a mesh: dp: 4 (over y, x), mp: 8 (over z, core).
Axes of the slice: x: 2, y: 2, z: 4, core: 2. Of those that a mesh axis runs over, the one named last changes fastest.
Arguments:
- queries: bfloat16 [32, 48, 2048], P('dp'), may hold values from -3 to 3
- new_keys: bfloat16 [32, 48, 2048], P('dp'), may hold values from -3 to 3
- new_values: bfloat16 [32, 48, 2048], P('dp'), may hold values from -6 to 6
- cache_keys: bfloat16 [32, 1024, 2048], P('dp', 'mp'), may hold values from -3 to 3
- cache_values: bfloat16 [32, 1024, 2048], P('dp', 'mp'), may hold values from -6 to 6
- lengths: int32 [32], P('dp'), may hold values from 16 to 1024, as said below
- parents: int32 [32, 48], P('dp'), may hold values from 0 to 46, as said below
- tree_tokens: int32 [32, 48], P('dp'), may hold values from 0 to 19455
- residual: bfloat16 [32, 48, 2048], P('dp'), may hold values from -6 to 6
- out_weight: bfloat16 [2048, 2048], P(('dp', 'mp')), may hold values from -0.125 to 0.125
- norm_gain: float32 [2048], replicated, may hold values from 0.25 to 1.75
- vocab_weight: bfloat16 [2048, 19456], P(None, 'mp'), may hold values from -0.375 to 0.375
Outputs:
- hidden: bfloat16 [32, 48, 2048], P('dp')
- node_logprob: float32 [32, 48], P('dp')
The draws below stay inside these ranges and needn't reach their ends.
Inputs may be any that keep to these rules, and one draw needn't show every extreme that they name: `lengths`: A request's cache length is 1024 or lies between 16 and 128; some request has length 1024 in every draw. parents[r, 0] is 0; for j > 0, parents[r, j] is j - 2 or j - 1 (0 for j = 1); some request's last node has parent 48 - 2 in every draw.
All inputs are finite; a program needn't handle non-finite values.
Results may differ from the reference program's by a relative error of at most 0.007.
Values may be sent and summed in bfloat16 or wider, within the bound.
A program may use at most 128 MiB of HBM per device.

```python
import jax
import jax.numpy as jnp
from jax import lax

D = 2048
HEADS = 16
HEAD_DIM = 128
TREE = 48
SINK = 4
REQUESTS = 32
CAP = 1024
WINDOW = 512
VOCAB = 19456


def draw_lengths(key, part):
    key_short = jax.random.fold_in(key, 11)
    key_flag = jax.random.fold_in(key, 12)
    key_pick = jax.random.fold_in(key, 13)
    short = jax.random.randint(key_short, (REQUESTS,), CAP // 64, CAP // 8 + 1)
    flagged = jax.random.randint(key_flag, (REQUESTS,), 0, 8) == 0
    chosen = jax.random.randint(key_pick, (), 0, REQUESTS)
    flagged = flagged | (jnp.arange(REQUESTS, dtype=jnp.int32) == chosen)
    return jnp.where(flagged, CAP, short).astype(jnp.int32)


def draw_parents(key, part):
    nodes = jnp.arange(TREE, dtype=jnp.int32)
    lower = jnp.maximum(nodes - 2, 0)
    upper = jnp.maximum(nodes, 1)
    drawn = jax.random.randint(jax.random.fold_in(key, 21), (REQUESTS, TREE), lower[None, :], upper[None, :])
    rows = jnp.arange(REQUESTS, dtype=jnp.int32)[:, None]
    fixed = (rows == 0) & (nodes[None, :] == TREE - 1)
    drawn = jnp.where(fixed, TREE - 2, drawn)
    return drawn.astype(jnp.int32)


def set_ends(array, stream_key, smallest, high):
    dims = array.shape
    spot = [jax.random.randint(jax.random.fold_in(stream_key, axis), (), 0, dims[axis]) for axis in range(len(dims))]
    array = array.at[tuple(spot)].set(smallest)
    longest = dims.index(max(dims))
    spot[longest] = (spot[longest] + 1) % dims[longest]
    return array.at[tuple(spot)].set(high)


def level_of(rng, extent, pieces, least, high):
    gain = 1.0
    for axis_at, parts in pieces:
        draws = jax.random.uniform(jax.random.fold_in(jax.random.fold_in(rng, 6), axis_at), (parts,), jnp.float32, least / len(pieces), high / len(pieces))
        gain = gain * jnp.repeat(jnp.exp(draws), extent[axis_at] // parts).reshape((-1,) + (1,) * (len(extent) - 1 - axis_at))
    return gain


def gaussian(key, shape, spread, reach, shards=(), kind=jnp.bfloat16):
    values = jax.random.normal(key, shape, jnp.float32) * spread
    if len(shards) > 0:
        values = level_of(key, shape, shards, -0.22, 0.18) * values
    return jnp.clip(values, min=-reach, max=reach).astype(kind)


def setup_inputs(seed: int = 0) -> dict:
    splits = jax.random.split(jax.random.key(seed), 13)
    queries = gaussian(splits[0], (REQUESTS, TREE, D), 1.0, 3.0, ((0, 4),))
    new_keys = gaussian(splits[1], (REQUESTS, TREE, D), 1.0, 3.0, ((0, 4),))
    new_values = gaussian(splits[2], (REQUESTS, TREE, D), 1.0, 6.0, ((0, 4),))
    cache_keys = gaussian(splits[3], (REQUESTS, CAP, D), 1.0, 3.0, ((0, 4), (1, 8)))
    cache_values = gaussian(splits[4], (REQUESTS, CAP, D), 1.0, 6.0, ((0, 4), (1, 8)))
    lengths = draw_lengths(jax.random.fold_in(splits[12], 71), 0)
    parents = draw_parents(jax.random.fold_in(splits[12], 71), 0)
    tree_tokens = set_ends(jax.random.randint(splits[7], (REQUESTS, TREE), 0, VOCAB), jax.random.fold_in(splits[7], 1), 0, VOCAB - 1).astype(jnp.int32)
    residual = gaussian(splits[8], (REQUESTS, TREE, D), 1.0, 6.0, ((0, 4),))
    out_weight = gaussian(splits[9], (D, D), D ** -0.5, 0.125, ((0, 32),))
    norm_gain = jnp.clip(1.0 + 0.15 * jax.random.normal(splits[10], (D,), jnp.float32), 0.25, 1.75)
    vocab_weight = gaussian(splits[11], (D, VOCAB), (D // 9) ** -0.5, 0.375, ((1, 8),))
    return dict(queries=queries, new_keys=new_keys, new_values=new_values, cache_keys=cache_keys, cache_values=cache_values, lengths=lengths, parents=parents, tree_tokens=tree_tokens, residual=residual, out_weight=out_weight, norm_gain=norm_gain, vocab_weight=vocab_weight)


def ancestor_mask(parents):
    tree = parents.shape[-1]
    idx = jnp.arange(tree, dtype=jnp.int32)
    links = ((idx[None, :, None] == idx[None, None, :]) | (parents[:, :, None] == idx[None, None, :])).astype(jnp.float32)
    for _ in range((tree - 1).bit_length()):
        links = jnp.minimum(jnp.einsum('rij,rjk->rik', links, links, precision=lax.Precision.HIGHEST), 1.0)
    return links > 0.5

def reference(queries, new_keys, new_values, cache_keys, cache_values, lengths, parents, tree_tokens, residual, out_weight, norm_gain, vocab_weight):
    scale = HEAD_DIM ** (-0.5)
    ancestors = ancestor_mask(parents)
    positions = jnp.arange(CAP, dtype=jnp.int32)

    def one_request(items):
        query, nkey, nval, ckey, cval, length, anc = items
        q4 = query.reshape(TREE, HEADS, HEAD_DIM).astype(jnp.float32)
        k4 = ckey.reshape(CAP, HEADS, HEAD_DIM).astype(jnp.float32)
        v4 = cval.reshape(CAP, HEADS, HEAD_DIM).astype(jnp.float32)
        nk4 = nkey.reshape(TREE, HEADS, HEAD_DIM).astype(jnp.float32)
        nv4 = nval.reshape(TREE, HEADS, HEAD_DIM).astype(jnp.float32)
        visible = (positions < length) & ((positions < SINK) | (positions >= length - WINDOW))
        cache_e = jnp.where(visible[None, None, :], jnp.exp(jnp.einsum('ihd,shd->his', q4, k4) * scale), 0.0)
        tree_e = jnp.where(anc[None], jnp.exp(jnp.einsum('ihd,jhd->hij', q4, nk4) * scale), 0.0)
        denom = lax.optimization_barrier(jnp.sum(cache_e, -1)) + lax.optimization_barrier(jnp.sum(tree_e, -1))
        cache_r = lax.optimization_barrier(cache_e.astype(jnp.bfloat16)).astype(jnp.float32)
        tree_r = lax.optimization_barrier(tree_e.astype(jnp.bfloat16)).astype(jnp.float32)
        numer = jnp.einsum('his,shd->ihd', cache_r, v4) + jnp.einsum('hij,jhd->ihd', tree_r, nv4)
        return (numer / jnp.transpose(denom)[:, :, None]).reshape(TREE, D).astype(jnp.bfloat16)
    attended = lax.map(one_request, (queries, new_keys, new_values, cache_keys, cache_values, lengths, ancestors))
    flat = attended.reshape(REQUESTS * TREE, D)
    projected = jnp.dot(flat, out_weight, preferred_element_type=jnp.float32)
    hidden = (residual.reshape(REQUESTS * TREE, D).astype(jnp.float32) + projected).astype(jnp.bfloat16)
    hfloat = hidden.astype(jnp.float32)
    normed = (hfloat * lax.rsqrt(lax.optimization_barrier(jnp.mean(hfloat * hfloat, -1, keepdims=True)) + 1e-06) * norm_gain).astype(jnp.bfloat16)
    normed = normed.reshape(REQUESTS, TREE, D)

    def score_request(items):
        rows, par, toks = items
        logits = jnp.dot(rows, vocab_weight, preferred_element_type=jnp.float32)
        total = lax.optimization_barrier(jnp.sum(jnp.exp(logits), -1))
        return logits[par, toks] - jnp.log(total[par])
    node_logprob = lax.map(score_request, (normed, parents, tree_tokens))
    return (hidden.reshape(REQUESTS, TREE, D), node_logprob)
```

```python
import functools

import jax
import jax.numpy as jnp
from jax import lax
from jax.experimental import pallas as pl
from jax.experimental.pallas import tpu as pltpu
from jax.sharding import PartitionSpec as P

HEADS = 16
SINK = 4
F32 = jnp.float32
BF16 = jnp.bfloat16
MESH = pl.DeviceIdType.MESH
VMEM_LIMIT = 50 * 1024 * 1024


def ancestor_mask(parents):
    tree = parents.shape[-1]
    idx = jnp.arange(tree, dtype=jnp.int32)
    links = (
        (idx[None, :, None] == idx[None, None, :]) | (parents[:, :, None] == idx[None, None, :])
    ).astype(F32)
    for _ in range((tree - 1).bit_length()):
        links = jnp.minimum(
            jnp.einsum("rij,rjk->rik", links, links, precision=lax.Precision.HIGHEST), 1.0
        )
    return links > 0.5


def attention_kernel(shards, len_ref, q_ref, k_ref, v_ref, nk_ref, nv_ref, anc_ref, o_ref):
    req = pl.program_id(0)
    shard = lax.axis_index("mp")
    slots = k_ref.shape[1]
    tree, width = q_ref.shape[1:]
    hd = width // HEADS
    scale = hd ** (-0.5)
    cap = slots * shards
    length = len_ref[req]
    start = shard * slots
    tree_shard = max(shards // 8, 1)
    seen = (start < length) & ((start < SINK) | (start + slots > length - cap // 2))

    def attend(keys, values, mask):
        lane = lax.broadcasted_iota(jnp.int32, (tree, 128), 1)
        den = jnp.zeros((tree, 128), F32)
        for h in range(HEADS):
            cols = slice(h * hd, (h + 1) * hd)
            s = lax.dot_general(
                q_ref[0, :, cols], keys[0, :, cols], (((1,), (1,)), ((), ())),
                preferred_element_type=F32,
            )
            e = jnp.where(mask, jnp.exp(s * scale), 0.0)
            den = jnp.where(lane == h, jnp.sum(e, -1, keepdims=True), den)
            o_ref[0, :, cols] = jnp.dot(
                e.astype(BF16), values[0, :, cols], preferred_element_type=F32
            ).astype(BF16)
        o_ref[0, :, width:] = den.astype(BF16)

    @pl.when(shard == tree_shard)
    def _():
        attend(nk_ref, nv_ref, anc_ref[0] > 0.5)

    @pl.when((shard != tree_shard) & seen)
    def _():
        pos = start + lax.broadcasted_iota(jnp.int32, (tree, slots), 1)
        attend(
            k_ref, v_ref, (pos < length) & ((pos < SINK) | (pos >= length - cap // 2))
        )

    @pl.when((shard != tree_shard) & jnp.logical_not(seen))
    def _():
        o_ref[...] = jnp.zeros_like(o_ref)


def attention(shards, queries, new_keys, new_values, cache_keys, cache_values, lengths, anc):
    reqs, tree, width = queries.shape
    slots = cache_keys.shape[1]

    def block(rows, cols):
        return pl.BlockSpec((1, rows, cols), lambda r: (r, 0, 0))

    return pl.pallas_call(
        functools.partial(attention_kernel, shards),
        grid=(reqs,),
        in_specs=[
            pl.BlockSpec(memory_space=pltpu.SMEM),
            block(tree, width),
            block(slots, width),
            block(slots, width),
            block(tree, width),
            block(tree, width),
            block(tree, tree),
        ],
        out_specs=block(tree, width + 128),
        out_shape=jax.ShapeDtypeStruct((reqs, tree, width + 128), BF16),
        compiler_params=pltpu.CompilerParams(vmem_limit_bytes=VMEM_LIMIT),
        name="attention_part",
    )(lengths, queries, cache_keys, cache_values, new_keys, new_values, anc)


def when(cond, fn):
    pl.when(cond)(fn)


def gather_line(chips, buf, recv, send_r, send_l, send_s):
    me = lax.axis_index("mp")
    c, z = lax.rem(me, 2), lax.div(me, 2)
    sib = 2 * z + 1 - c

    def copy(slot, sem, to):
        return pltpu.make_async_remote_copy(
            src_ref=buf.at[slot], dst_ref=buf.at[slot], send_sem=sem, recv_sem=recv.at[slot],
            device_id={"mp": to}, device_id_type=MESH,
        )

    def right(k):
        return copy(2 * (z - k) + c, send_r.at[k], me + 2)

    def left(k):
        return copy(2 * (z + k) + c, send_l.at[k], me - 2)

    def pair(zs):
        return copy(2 * zs + c, send_s.at[zs], sib)

    when(z < chips - 1, lambda: right(0).start())
    when(z > 0, lambda: left(0).start())
    pair(z).start()
    for k in range(1, chips):

        @pl.when(z - k >= 0)
        def _():
            right(k).wait_recv()
            when(z < chips - 1, lambda: right(k).start())
            pair(z - k).start()

        @pl.when(z + k <= chips - 1)
        def _():
            left(k).wait_recv()
            when(z > 0, lambda: left(k).start())
            pair(z + k).start()

    for zs in range(chips):
        copy(2 * zs + 1 - c, send_s.at[zs], sib).wait_recv()

    def finish():
        for k in range(chips):
            when((z - k >= 0) & (z < chips - 1), lambda: right(k).wait_send())
            when((z + k <= chips - 1) & (z > 0), lambda: left(k).wait_send())
        for zs in range(chips):
            pair(zs).wait_send()

    return finish


def hidden_kernel(
    chips, groups, part, w_ref, res_ref, out_ref,
    sib_buf, from_l, from_r, acc, tot, att, wcol, hcol,
    sib_s, sib_r, fl_r, fr_r, acc_s, g1_r, g1_a, g1_b, g1_c, g2_r, g2_a, g2_b, g2_c,
    w1_s, w1_r, w2_s, w2_r, own_s,
):
    shards = 2 * chips
    me = lax.axis_index("mp")
    grp = lax.axis_index("dp")
    c, z = lax.rem(me, 2), lax.div(me, 2)
    sib = 2 * z + 1 - c
    width = att.shape[-1]
    hd = width // HEADS
    ncol = wcol.shape[-1]

    barrier = pltpu.get_barrier_semaphore()
    for k in range(1, shards):
        pl.semaphore_signal(
            barrier, inc=1, device_id={"mp": lax.rem(me + k, shards)}, device_id_type=MESH
        )
    for k in range(1, groups):
        pl.semaphore_signal(
            barrier, inc=1, device_id={"dp": lax.rem(grp + k, groups)}, device_id_type=MESH
        )
    pl.semaphore_wait(barrier, shards - 1 + groups - 1)

    def pair(zd):
        return pltpu.make_async_remote_copy(
            src_ref=part.at[2 * zd + 1 - c], dst_ref=sib_buf.at[zd], send_sem=sib_s.at[zd],
            recv_sem=sib_r.at[zd], device_id={"mp": sib}, device_id_type=MESH,
        )

    order = []
    for k in range(chips):
        for zd in (chips - 1 - k, k):
            if zd not in order:
                order.append(zd)
    for zd in order:
        pair(zd).start()

    def columns(j):
        return pl.ds(pl.multiple_of(j * ncol, 128), ncol)

    def w_mp(k):
        to = lax.rem(me + k, shards)
        return pltpu.make_async_remote_copy(
            src_ref=w_ref.at[:, columns(to)], dst_ref=wcol.at[grp, me], send_sem=w1_s.at[k],
            recv_sem=w1_r.at[k], device_id={"mp": to}, device_id_type=MESH,
        )

    for k in range(1, shards):
        w_mp(k).start()
    own = pltpu.make_async_copy(w_ref.at[:, columns(me)], wcol.at[grp, me], own_s)
    own.start()

    def pass_on(zd, buf, sems, to):
        return pltpu.make_async_remote_copy(
            src_ref=acc.at[zd], dst_ref=buf.at[zd], send_sem=acc_s.at[zd],
            recv_sem=sems.at[zd], device_id={"mp": to}, device_id_type=MESH,
        )

    def both(zd):
        return part[2 * zd + c].astype(F32) + sib_buf[zd].astype(F32)

    def step(zd, buf, sems, first, to):
        pair(zd).wait_recv()

        @pl.when(first)
        def _():
            acc[zd] = both(zd).astype(BF16)

        @pl.when(jnp.logical_not(first))
        def _():
            pass_on(zd, buf, sems, to).wait_recv()
            acc[zd] = (both(zd) + buf[zd].astype(F32)).astype(BF16)

        pass_on(zd, buf, sems, to).start()

    for k in range(chips - 1):
        rd, ld = chips - 1 - k, k
        when(rd > z, functools.partial(step, rd, from_l, fl_r, z == 0, me + 2))
        when(ld < z, functools.partial(step, ld, from_r, fr_r, z == chips - 1, me - 2))

    pair(z).wait_recv()
    tot[...] = both(z)

    @pl.when(z > 0)
    def _():
        pass_on(z, from_l, fl_r, me).wait_recv()
        tot[...] += from_l[z].astype(F32)

    @pl.when(z < chips - 1)
    def _():
        pass_on(z, from_r, fr_r, me).wait_recv()
        tot[...] += from_r[z].astype(F32)

    for h in range(HEADS):
        cols = slice(h * hd, (h + 1) * hd)
        att[me, :, cols] = (tot[:, cols] / tot[:, width + h : width + h + 1]).astype(BF16)

    for k in range(1, shards):
        w_mp(k).wait_recv()
    own.wait()

    def w_dp(k, src):
        return pltpu.make_async_remote_copy(
            src_ref=wcol.at[src], dst_ref=wcol.at[src], send_sem=w2_s.at[k],
            recv_sem=w2_r.at[k], device_id={"dp": lax.rem(grp + k, groups)}, device_id_type=MESH,
        )

    for k in range(1, groups):
        w_dp(k, grp).start()

    done_1 = gather_line(chips, att, g1_r, g1_a, g1_b, g1_c)
    for k in range(1, groups):
        w_dp(k, lax.rem(grp + groups - k, groups)).wait_recv()

    rows = att.shape[0] * att.shape[1]
    projected = jnp.dot(
        att[...].reshape(rows, width), wcol[...].reshape(width, ncol), preferred_element_type=F32
    )
    hcol[me] = (res_ref[...].astype(F32) + projected).astype(BF16)
    done_2 = gather_line(chips, hcol, g2_r, g2_a, g2_b, g2_c)
    for j in range(shards):
        out_ref[:, j * ncol : (j + 1) * ncol] = hcol[j]

    done_1()
    done_2()
    for zd in range(chips):
        pair(zd).wait_send()
        when(zd != z, lambda: pass_on(zd, from_l, fl_r, me).wait_send())
    for k in range(1, shards):
        w_mp(k).wait_send()
    for k in range(1, groups):
        w_dp(k, grp).wait_send()


def hidden_of(shards, groups, part, out_weight, res):
    own, width = part.shape[1], out_weight.shape[1]
    wide = part.shape[2]
    tokens = own * shards
    ncol = width // shards
    chips = shards // 2
    dma = pltpu.SemaphoreType.DMA
    gather_sems = [dma((shards,)), dma((chips,)), dma((chips,)), dma((chips,))]
    vmem = pl.BlockSpec(memory_space=pltpu.VMEM)
    return pl.pallas_call(
        functools.partial(hidden_kernel, chips, groups),
        in_specs=[vmem] * 3,
        out_specs=vmem,
        out_shape=jax.ShapeDtypeStruct((tokens, width), BF16),
        scratch_shapes=[
            pltpu.VMEM((chips, own, wide), BF16),
            pltpu.VMEM((chips, own, wide), BF16),
            pltpu.VMEM((chips, own, wide), BF16),
            pltpu.VMEM((chips, own, wide), BF16),
            pltpu.VMEM((own, wide), F32),
            pltpu.VMEM((shards, own, width), BF16),
            pltpu.VMEM((groups, shards, out_weight.shape[0], ncol), BF16),
            pltpu.VMEM((shards, tokens, ncol), BF16),
            dma((chips,)), dma((chips,)), dma((chips,)), dma((chips,)), dma((chips,)),
            *gather_sems,
            *gather_sems,
            dma((shards,)), dma((shards,)), dma((groups,)), dma((groups,)), dma,
        ],
        compiler_params=pltpu.CompilerParams(
            collective_id=0, has_side_effects=True, vmem_limit_bytes=VMEM_LIMIT
        ),
        name="hidden_exchange",
    )(part, out_weight, res)


def score_kernel(vocab, h_ref, g_ref, t_ref, w_ref, o_ref, normed, sums):
    step = pl.program_id(0)
    tile = w_ref.shape[1]
    rows = h_ref.shape[0]

    @pl.when(step == 0)
    def _():
        h = h_ref[...].astype(F32)
        normed[...] = (
            h * lax.rsqrt(jnp.mean(h * h, -1, keepdims=True) + 1e-06) * g_ref[...]
        ).astype(BF16)
        sums[...] = jnp.zeros_like(sums)

    logits = jnp.dot(normed[...], w_ref[...], preferred_element_type=F32)
    lane = lax.broadcasted_iota(jnp.int32, (rows, 128), 1)
    marks = [t_ref[:, n : n + 1] for n in range(3)]
    new = [jnp.zeros((rows, 128), F32) for _ in range(4)]
    for b in range(tile // 128):
        col = step * tile + b * 128 + lane
        x = logits[:, b * 128 : (b + 1) * 128]
        new[0] += jnp.where(col < vocab, jnp.exp(x), 0.0)
        for n in range(3):
            new[n + 1] += jnp.where(col == marks[n], x, 0.0)
    for n in range(4):
        sums[n] += new[n]

    @pl.when(step == pl.num_programs(0) - 1)
    def _():
        stat = jnp.zeros((rows, 128), F32)
        for n in range(4):
            stat = jnp.where(lane == n, jnp.sum(sums[n], -1, keepdims=True), stat)
        o_ref[...] = jnp.transpose(stat)[:8]


def score(hidden, gain, marks, vocab_weight):
    rows, width = hidden.shape
    vocab = vocab_weight.shape[1]
    tile = 512
    return pl.pallas_call(
        functools.partial(score_kernel, vocab),
        grid=(pl.cdiv(vocab, tile),),
        in_specs=[
            pl.BlockSpec((rows, width), lambda i: (0, 0)),
            pl.BlockSpec((1, width), lambda i: (0, 0)),
            pl.BlockSpec((rows, 128), lambda i: (0, 0)),
            pl.BlockSpec((width, tile), lambda i: (0, i)),
        ],
        out_specs=pl.BlockSpec((8, rows), lambda i: (0, 0)),
        out_shape=jax.ShapeDtypeStruct((8, rows), F32),
        scratch_shapes=[pltpu.VMEM((rows, width), BF16), pltpu.VMEM((4, rows, 128), F32)],
        compiler_params=pltpu.CompilerParams(vmem_limit_bytes=VMEM_LIMIT),
        name="score_part",
    )(hidden, gain, marks, vocab_weight)


def total_kernel(shards, x_ref, o_ref, slots, send, recv):
    me = lax.axis_index("mp")
    barrier = pltpu.get_barrier_semaphore()
    for k in range(1, shards):
        pl.semaphore_signal(
            barrier, inc=1, device_id={"mp": lax.rem(me + k, shards)}, device_id_type=MESH
        )
    pl.semaphore_wait(barrier, shards - 1)

    def copy(k):
        return pltpu.make_async_remote_copy(
            src_ref=x_ref, dst_ref=slots.at[k], send_sem=send.at[k], recv_sem=recv.at[k],
            device_id={"mp": lax.rem(me + k, shards)}, device_id_type=MESH,
        )

    for k in range(1, shards):
        copy(k).start()
    total = x_ref[...]
    for k in range(1, shards):
        copy(k).wait_recv()
        total = total + slots[k]
    o_ref[...] = total
    for k in range(1, shards):
        copy(k).wait_send()


def total_of(shards, stats):
    vmem = pl.BlockSpec(memory_space=pltpu.VMEM)
    dma = pltpu.SemaphoreType.DMA
    return pl.pallas_call(
        functools.partial(total_kernel, shards),
        in_specs=[vmem],
        out_specs=vmem,
        out_shape=jax.ShapeDtypeStruct(stats.shape, F32),
        scratch_shapes=[
            pltpu.VMEM((shards,) + stats.shape, F32), dma((shards,)), dma((shards,)),
        ],
        compiler_params=pltpu.CompilerParams(collective_id=1, has_side_effects=True),
        name="total_exchange",
    )(stats)


def local_fast(
    queries, new_keys, new_values, cache_keys, cache_values, lengths, parents, tree_tokens,
    residual, out_weight, norm_gain, vocab_weight,
):
    reqs, tree, width = queries.shape
    tokens = reqs * tree
    shard = lax.axis_index("mp")
    shards = lax.axis_size("mp")
    groups = lax.axis_size("dp")
    ncol = width // shards
    anc = ancestor_mask(parents).astype(F32)
    part = attention(
        shards, queries, new_keys, new_values, cache_keys, cache_values, lengths, anc
    ).reshape(shards, tokens // shards, width + 128)
    res = lax.dynamic_slice_in_dim(residual.reshape(tokens, width), shard * ncol, ncol, 1)
    hidden = hidden_of(shards, groups, part, out_weight, res)

    vocab = vocab_weight.shape[1]
    column = tree_tokens - shard * vocab
    column = jnp.where((column >= 0) & (column < vocab), column, -1)
    idx = jnp.arange(tree, dtype=jnp.int32)[None, :]
    by_one = (parents == idx - 1) & (idx > 0)
    by_two = (parents == idx - 2) & (idx > 1)

    def ahead(x, n):
        return jnp.pad(x[:, n:], ((0, 0), (0, n)), constant_values=-1)

    first = jnp.where(idx == 0, column, -1)
    marks = jnp.stack(
        [ahead(jnp.where(by_one, column, -1), 1), ahead(jnp.where(by_two, column, -1), 2), first], -1
    ).reshape(tokens, 3)
    marks = jnp.pad(marks, ((0, 0), (0, 125)), constant_values=-1)
    stats = score(hidden, norm_gain.reshape(1, width), marks, vocab_weight)
    total = total_of(shards, stats).reshape(8, reqs, tree)

    def behind(x, n):
        return jnp.pad(x[:, : tree - n], ((0, 0), (n, 0)))

    sums = total[0]
    picked = jnp.where(idx == 0, total[3], jnp.where(by_one, behind(total[1], 1), behind(total[2], 2)))
    norm = jnp.where(idx == 0, sums, jnp.where(by_one, behind(sums, 1), behind(sums, 2)))
    return (hidden.reshape(reqs, tree, width), picked - jnp.log(norm))


def local_plain(
    queries,
    new_keys,
    new_values,
    cache_keys,
    cache_values,
    lengths,
    parents,
    tree_tokens,
    residual,
    out_weight,
    norm_gain,
    vocab_weight,
):
    reqs, tree, width = queries.shape
    slots = cache_keys.shape[1]
    head_dim = width // HEADS
    scale = head_dim ** (-0.5)
    shard = lax.axis_index("mp")
    shards = lax.axis_size("mp")
    tokens = reqs * tree
    window = slots * shards // 2
    positions = shard * slots + jnp.arange(slots, dtype=jnp.int32)
    visible = (positions[None, :] < lengths[:, None]) & (
        (positions[None, :] < SINK) | (positions[None, :] >= lengths[:, None] - window)
    )
    q4 = queries.reshape(reqs, tree, HEADS, head_dim)
    k4 = cache_keys.reshape(reqs, slots, HEADS, head_dim)
    v4 = cache_values.reshape(reqs, slots, HEADS, head_dim)
    cache_e = jnp.where(
        visible[:, None, None, :],
        jnp.exp(jnp.einsum("rihd,rshd->rhis", q4, k4, preferred_element_type=jnp.float32) * scale),
        0.0,
    )
    cache_den = jnp.sum(cache_e, -1)
    cache_num = jnp.einsum(
        "rhis,rshd->rihd", cache_e.astype(jnp.bfloat16), v4, preferred_element_type=jnp.float32
    )
    ancestors = ancestor_mask(parents)
    nk4 = new_keys.reshape(reqs, tree, HEADS, head_dim)
    nv4 = new_values.reshape(reqs, tree, HEADS, head_dim)
    tree_e = jnp.where(
        ancestors[:, None],
        jnp.exp(jnp.einsum("rihd,rjhd->rhij", q4, nk4, preferred_element_type=jnp.float32) * scale),
        0.0,
    )
    tree_den = jnp.sum(tree_e, -1)
    tree_num = jnp.einsum(
        "rhij,rjhd->rihd", tree_e.astype(jnp.bfloat16), nv4, preferred_element_type=jnp.float32
    )
    flat_res = residual.reshape(tokens, width)
    num_all, den_all = lax.psum((cache_num.reshape(tokens, width), cache_den), "mp")
    denom = jnp.transpose(den_all + tree_den, (0, 2, 1))
    numer = num_all.reshape(reqs, tree, HEADS, head_dim) + tree_num
    attended = (numer / denom[..., None]).astype(jnp.bfloat16).reshape(tokens, width)
    projected = jnp.dot(
        attended,
        lax.all_gather(out_weight, ("dp", "mp"), axis=0, tiled=True),
        preferred_element_type=jnp.float32,
    )
    hidden = (flat_res.astype(jnp.float32) + projected).astype(jnp.bfloat16)
    hfloat = hidden.astype(jnp.float32)
    normed = (
        hfloat * lax.rsqrt(jnp.mean(hfloat * hfloat, -1, keepdims=True) + 1e-06) * norm_gain
    ).astype(jnp.bfloat16)
    vocab_dev = vocab_weight.shape[1]
    logits = jnp.dot(normed, vocab_weight, preferred_element_type=jnp.float32)
    exp_sums = jnp.sum(jnp.exp(logits), -1)
    parent_rows = (jnp.arange(reqs, dtype=jnp.int32)[:, None] * tree + parents).reshape(-1)
    column = tree_tokens.reshape(-1) - shard * vocab_dev
    inside = (column >= 0) & (column < vocab_dev)
    picked = jnp.where(inside, logits[parent_rows, jnp.clip(column, 0, vocab_dev - 1)], 0.0)
    parent_sums = exp_sums[parent_rows]
    total_sums, total_picked = lax.psum((parent_sums, picked), "mp")
    node_logprob = (total_picked - jnp.log(total_sums)).reshape(reqs, tree)
    return (hidden.reshape(reqs, tree, width), node_logprob)


def local(*args):
    queries, vocab_weight = args[0], args[-1]
    reqs, tree, width = queries.shape
    shards = lax.axis_size("mp")
    fits = (
        (reqs * tree) % (shards * 16) == 0
        and width % (shards * 128) == 0
        and width == HEADS * 128
        and tree % 16 == 0
        and shards % 2 == 0
        and shards >= 8
    )
    return (local_fast if fits else local_plain)(*args)


def solution(mesh):
    placed = (
        P("dp", None, None),
        P("dp", None, None),
        P("dp", None, None),
        P("dp", "mp", None),
        P("dp", "mp", None),
        P("dp"),
        P("dp", None),
        P("dp", None),
        P("dp", None, None),
        P(("dp", "mp"), None),
        P(),
        P(None, "mp"),
    )
    return jax.shard_map(
        local,
        mesh=mesh,
        in_specs=placed,
        out_specs=(P("dp", None, None), P("dp", None)),
        check_vma=False,
    )
```

```python
import functools

import jax
import jax.numpy as jnp
from jax import lax
from jax.experimental import pallas as pl
from jax.experimental.pallas import tpu as pltpu
from jax.sharding import PartitionSpec as P

HEADS = 16
SINK = 4
F32 = jnp.float32
BF16 = jnp.bfloat16
MESH = pl.DeviceIdType.MESH
VMEM_LIMIT = 50 * 1024 * 1024


def ancestor_mask(parents):
    tree = parents.shape[-1]
    idx = jnp.arange(tree, dtype=jnp.int32)
    links = (
        (idx[None, :, None] == idx[None, None, :]) | (parents[:, :, None] == idx[None, None, :])
    ).astype(F32)
    for _ in range((tree - 1).bit_length()):
        links = jnp.minimum(
            jnp.einsum("rij,rjk->rik", links, links, precision=lax.Precision.HIGHEST), 1.0
        )
    return links > 0.5


def attention_kernel(
    shards, len_ref, q_ref, k_ref, v_ref, nk_ref, nv_ref, par_ref, o_ref, chain
):
    req = pl.program_id(0)
    shard = lax.axis_index("mp")
    slots = k_ref.shape[1]
    tree, width = q_ref.shape[1:]
    reqs = par_ref.shape[0]
    hd = width // HEADS
    scale = hd ** (-0.5)
    cap = slots * shards
    length = len_ref[req]
    start = shard * slots
    tree_shard = max(shards // 8, 1)
    seen = (start < length) & ((start < SINK) | (start + slots > length - cap // 2))

    def attend(keys, values, mask):
        lane = lax.broadcasted_iota(jnp.int32, (tree, 128), 1)
        low = lax.broadcasted_iota(jnp.int32, (tree, 2 * hd), 1) < hd
        mask2 = jnp.concatenate([mask, mask], 0)
        den = jnp.zeros((tree, 128), F32)
        pairs = HEADS // 2
        for group in range(0, pairs, 4):
            scores = []
            for p in range(group, group + 4):
                cols = slice(2 * p * hd, 2 * (p + 1) * hd)
                q = q_ref[0, :, cols]
                both = jnp.concatenate(
                    [jnp.where(low, q, jnp.zeros_like(q)), jnp.where(low, jnp.zeros_like(q), q)], 0
                )
                scores.append(
                    lax.dot_general(
                        both, keys[0, :, cols], (((1,), (1,)), ((), ())),
                        preferred_element_type=F32,
                    )
                )
            es = [jnp.where(mask2 > 0.5, jnp.exp(s * scale), 0.0) for s in scores]
            for n, e in enumerate(es):
                p = group + n
                cols = slice(2 * p * hd, 2 * (p + 1) * hd)
                num = jnp.dot(e.astype(BF16), values[0, :, cols], preferred_element_type=F32)
                o_ref[0, :, 2 * p * hd : (2 * p + 1) * hd] = num[:tree, :hd].astype(BF16)
                o_ref[0, :, (2 * p + 1) * hd : 2 * (p + 1) * hd] = num[tree:, hd:].astype(BF16)
                d = jnp.sum(e, -1, keepdims=True)
                den = jnp.where(lane == 2 * p, d[:tree], den)
                den = jnp.where(lane == 2 * p + 1, d[tree:], den)
        o_ref[0, :, width:] = den.astype(BF16)

    @pl.when((shard == tree_shard) & (req == 0))
    def _():
        node = lax.broadcasted_iota(jnp.int32, (reqs, 128), 1)
        rows = []
        for j in range(tree):
            row = jnp.where(node == j, 1.0, 0.0)
            if j == 1:
                row = row + rows[0]
            elif j > 1:
                row = row + jnp.where(par_ref[:, j : j + 1] == j - 1, rows[j - 1], rows[j - 2])
            rows.append(row)
            chain[j] = row

    @pl.when(shard == tree_shard)
    def _():
        attend(nk_ref, nv_ref, chain[:, req, :][:, :tree])

    @pl.when((shard != tree_shard) & seen)
    def _():
        pos = start + lax.broadcasted_iota(jnp.int32, (tree, slots), 1)
        mask = (pos < length) & ((pos < SINK) | (pos >= length - cap // 2))
        attend(k_ref, v_ref, jnp.where(mask, 1.0, 0.0))

    @pl.when((shard != tree_shard) & jnp.logical_not(seen))
    def _():
        o_ref[...] = jnp.zeros_like(o_ref)


def attention(shards, queries, new_keys, new_values, cache_keys, cache_values, lengths, parents):
    reqs, tree, width = queries.shape
    slots = cache_keys.shape[1]

    def block(rows, cols):
        return pl.BlockSpec((1, rows, cols), lambda r: (r, 0, 0))

    return pl.pallas_call(
        functools.partial(attention_kernel, shards),
        grid=(reqs,),
        in_specs=[
            pl.BlockSpec(memory_space=pltpu.SMEM),
            block(tree, width),
            block(slots, width),
            block(slots, width),
            block(tree, width),
            block(tree, width),
            pl.BlockSpec((reqs, tree), lambda r: (0, 0)),
        ],
        out_specs=block(tree, width + 128),
        out_shape=jax.ShapeDtypeStruct((reqs, tree, width + 128), BF16),
        scratch_shapes=[pltpu.VMEM((tree, reqs, 128), F32)],
        compiler_params=pltpu.CompilerParams(vmem_limit_bytes=VMEM_LIMIT),
        name="attention_part",
    )(lengths, queries, cache_keys, cache_values, new_keys, new_values, parents)


def when(cond, fn):
    pl.when(cond)(fn)


class Line:
    def __init__(self, chips, at, recv, send_r, send_l, send_s):
        me = lax.axis_index("mp")
        self.chips, self.at, self.recv = chips, at, recv
        self.sends = send_r, send_l, send_s
        self.me, self.c, self.z = me, lax.rem(me, 2), lax.div(me, 2)
        self.sib = 2 * self.z + 1 - self.c

    def copy(self, slot, sem, to):
        return pltpu.make_async_remote_copy(
            src_ref=self.at(slot), dst_ref=self.at(slot), send_sem=sem,
            recv_sem=self.recv.at[slot], device_id={"mp": to}, device_id_type=MESH,
        )

    def right(self, k):
        return self.copy(2 * (self.z - k) + self.c, self.sends[0].at[k], self.me + 2)

    def left(self, k):
        return self.copy(2 * (self.z + k) + self.c, self.sends[1].at[k], self.me - 2)

    def pair(self, zs):
        return self.copy(2 * zs + self.c, self.sends[2].at[zs], self.sib)

    def start(self):
        when(self.z < self.chips - 1, lambda: self.right(0).start())
        when(self.z > 0, lambda: self.left(0).start())
        self.pair(self.z).start()

    def forward(self):
        z, chips = self.z, self.chips
        for k in range(1, chips):

            @pl.when(z - k >= 0)
            def _():
                self.right(k).wait_recv()
                when(z < chips - 1, lambda: self.right(k).start())
                self.pair(z - k).start()

            @pl.when(z + k <= chips - 1)
            def _():
                self.left(k).wait_recv()
                when(z > 0, lambda: self.left(k).start())
                self.pair(z + k).start()

        for zs in range(chips):
            self.copy(2 * zs + 1 - self.c, self.sends[2].at[zs], self.sib).wait_recv()

    def finish(self):
        z, chips = self.z, self.chips
        for k in range(chips):
            when((z - k >= 0) & (z < chips - 1), lambda: self.right(k).wait_send())
            when((z + k <= chips - 1) & (z > 0), lambda: self.left(k).wait_send())
        for zs in range(chips):
            self.pair(zs).wait_send()


CHUNK = 16


def hidden_kernel(
    chips, groups, part, w_ref, res_ref, out_ref,
    own_buf, sib_buf, from_l, from_r, acc, tot, att, wcol, hcol,
    own_s, sib_s, sib_r, fl_r, fr_r, acc_s, g1_r, g1_a, g1_b, g1_c, g2_r, g2_a, g2_b, g2_c,
    w1_s, w1_r, w2_s, w2_r, wown_s,
):
    shards = 2 * chips
    me = lax.axis_index("mp")
    grp = lax.axis_index("dp")
    c, z = lax.rem(me, 2), lax.div(me, 2)
    sib = 2 * z + 1 - c
    width = att.shape[-1]
    hd = width // HEADS
    ncol = wcol.shape[-1]
    chunks = att.shape[1] // CHUNK

    def rows(i):
        return pl.ds(i * CHUNK, CHUNK)

    def columns(j):
        return pl.ds(pl.multiple_of(j * ncol, 128), ncol)

    barrier = pltpu.get_barrier_semaphore()
    for k in range(1, shards):
        pl.semaphore_signal(
            barrier, inc=1, device_id={"mp": lax.rem(me + k, shards)}, device_id_type=MESH
        )
    for k in range(1, groups):
        pl.semaphore_signal(
            barrier, inc=1, device_id={"dp": lax.rem(grp + k, groups)}, device_id_type=MESH
        )

    order = []
    for k in range(chips):
        for zd in (chips - 1 - k, k):
            if zd not in order:
                order.append(zd)

    def mine(i, zd):
        return pltpu.make_async_copy(
            part.at[2 * zd + c, rows(i)], own_buf.at[zd, rows(i)], own_s.at[i, zd]
        )

    for i in range(chunks):
        for zd in order:
            mine(i, zd).start()
    own_w = pltpu.make_async_copy(w_ref.at[:, columns(me)], wcol.at[grp, me], wown_s)
    own_w.start()

    pl.semaphore_wait(barrier, shards - 1 + groups - 1)

    def pair(i, zd):
        return pltpu.make_async_remote_copy(
            src_ref=part.at[2 * zd + 1 - c, rows(i)], dst_ref=sib_buf.at[zd, rows(i)],
            send_sem=sib_s.at[i, zd], recv_sem=sib_r.at[i, zd],
            device_id={"mp": sib}, device_id_type=MESH,
        )

    for i in range(chunks):
        for zd in order:
            pair(i, zd).start()

    def w_mp(k):
        to = lax.rem(me + k, shards)
        return pltpu.make_async_remote_copy(
            src_ref=w_ref.at[:, columns(to)], dst_ref=wcol.at[grp, me], send_sem=w1_s.at[k],
            recv_sem=w1_r.at[k], device_id={"mp": to}, device_id_type=MESH,
        )

    def w_dp(k, src):
        return pltpu.make_async_remote_copy(
            src_ref=wcol.at[src], dst_ref=wcol.at[src], send_sem=w2_s.at[k],
            recv_sem=w2_r.at[k], device_id={"dp": lax.rem(grp + k, groups)}, device_id_type=MESH,
        )

    def pass_on(i, zd, buf, sems, to):
        return pltpu.make_async_remote_copy(
            src_ref=acc.at[zd, rows(i)], dst_ref=buf.at[zd, rows(i)], send_sem=acc_s.at[i, zd],
            recv_sem=sems.at[i, zd], device_id={"mp": to}, device_id_type=MESH,
        )

    def both(i, zd):
        return own_buf[zd, rows(i)].astype(F32) + sib_buf[zd, rows(i)].astype(F32)

    def arrive(i, zd):
        mine(i, zd).wait()
        pair(i, zd).wait_recv()

    def step(i, zd, buf, sems, first, to):
        arrive(i, zd)

        @pl.when(first)
        def _():
            acc[zd, rows(i)] = both(i, zd).astype(BF16)

        @pl.when(jnp.logical_not(first))
        def _():
            pass_on(i, zd, buf, sems, to).wait_recv()
            acc[zd, rows(i)] = (both(i, zd) + buf[zd, rows(i)].astype(F32)).astype(BF16)

        pass_on(i, zd, buf, sems, to).start()

    def sums(i):
        for k in range(chips - 1):
            rd, ld = chips - 1 - k, k
            when(rd > z, functools.partial(step, i, rd, from_l, fl_r, z == 0, me + 2))
            when(ld < z, functools.partial(step, i, ld, from_r, fr_r, z == chips - 1, me - 2))

    first = [
        Line(chips, lambda j, i=i: att.at[j, rows(i)], g1_r.at[i], g1_a.at[i], g1_b.at[i], g1_c.at[i])
        for i in range(chunks)
    ]
    second = [
        Line(chips, lambda j, i=i: hcol.at[j, i], g2_r.at[i], g2_a.at[i], g2_b.at[i], g2_c.at[i])
        for i in range(chunks)
    ]

    def attended(i):
        arrive(i, z)
        tot[...] = both(i, z)

        @pl.when(z > 0)
        def _():
            pass_on(i, z, from_l, fl_r, me).wait_recv()
            tot[...] += from_l[z, rows(i)].astype(F32)

        @pl.when(z < chips - 1)
        def _():
            pass_on(i, z, from_r, fr_r, me).wait_recv()
            tot[...] += from_r[z, rows(i)].astype(F32)

        for h in range(HEADS):
            cols = slice(h * hd, (h + 1) * hd)
            att[me, rows(i), cols] = (tot[:, cols] / tot[:, width + h : width + h + 1]).astype(BF16)
        first[i].start()

    def project(i):
        first[i].forward()
        if i == 0:
            for k in range(1, groups):
                w_dp(k, lax.rem(grp + groups - k, groups)).wait_recv()
        projected = jnp.dot(
            att[:, rows(i), :].reshape(shards * CHUNK, width),
            wcol[...].reshape(width, ncol),
            preferred_element_type=F32,
        )
        res = res_ref[:, rows(i), :].reshape(shards * CHUNK, ncol)
        hcol[me, i] = (res.astype(F32) + projected).astype(BF16)
        second[i].start()

    def place(i):
        second[i].forward()
        for j in range(shards):
            for t in range(shards):
                out_ref[t, rows(i), j * ncol : (j + 1) * ncol] = hcol[
                    j, i, t * CHUNK : (t + 1) * CHUNK
                ]

    sums(0)
    for k in range(1, shards):
        w_mp(k).start()
    for i in range(chunks):
        if i + 1 < chunks:
            sums(i + 1)
        attended(i)
        if i == 0:
            for k in range(1, shards):
                w_mp(k).wait_recv()
            own_w.wait()
            for k in range(1, groups):
                w_dp(k, grp).start()
        if i >= 1:
            project(i - 1)
        if i >= 2:
            place(i - 2)
    project(chunks - 1)
    if chunks >= 2:
        place(chunks - 2)
    place(chunks - 1)

    for i in range(chunks):
        first[i].finish()
        second[i].finish()
        for zd in range(chips):
            pair(i, zd).wait_send()
            when(zd != z, lambda: pass_on(i, zd, from_l, fl_r, me).wait_send())
    for k in range(1, shards):
        w_mp(k).wait_send()
    for k in range(1, groups):
        w_dp(k, grp).wait_send()


def hidden_of(shards, groups, part, out_weight, res):
    own, width = part.shape[1], out_weight.shape[1]
    wide = part.shape[2]
    ncol = width // shards
    chips = shards // 2
    chunks = own // CHUNK
    dma = pltpu.SemaphoreType.DMA
    gather_sems = [dma((chunks, shards))] + [dma((chunks, chips))] * 3
    vmem = pl.BlockSpec(memory_space=pltpu.VMEM)
    return pl.pallas_call(
        functools.partial(hidden_kernel, chips, groups),
        in_specs=[pl.BlockSpec(memory_space=pl.ANY), vmem, vmem],
        out_specs=vmem,
        out_shape=jax.ShapeDtypeStruct((shards, own, width), BF16),
        scratch_shapes=[
            pltpu.VMEM((chips, own, wide), BF16),
            pltpu.VMEM((chips, own, wide), BF16),
            pltpu.VMEM((chips, own, wide), BF16),
            pltpu.VMEM((chips, own, wide), BF16),
            pltpu.VMEM((chips, own, wide), BF16),
            pltpu.VMEM((CHUNK, wide), F32),
            pltpu.VMEM((shards, own, width), BF16),
            pltpu.VMEM((groups, shards, out_weight.shape[0], ncol), BF16),
            pltpu.VMEM((shards, chunks, shards * CHUNK, ncol), BF16),
            *[dma((chunks, chips))] * 6,
            *gather_sems,
            *gather_sems,
            dma((shards,)), dma((shards,)), dma((groups,)), dma((groups,)), dma,
        ],
        compiler_params=pltpu.CompilerParams(
            collective_id=0, has_side_effects=True, vmem_limit_bytes=VMEM_LIMIT
        ),
        name="hidden_exchange",
    )(part, out_weight, res)


def score_kernel(vocab, shards, h_ref, g_ref, t_ref, w_ref, o_ref, normed, sums, stats, slots, send, recv):
    step = pl.program_id(0)
    tile = w_ref.shape[1]
    rows = h_ref.shape[0]
    me = lax.axis_index("mp")
    barrier = pltpu.get_barrier_semaphore()

    @pl.when(step == 0)
    def _():
        for k in range(1, shards):
            pl.semaphore_signal(
                barrier, inc=1, device_id={"mp": lax.rem(me + k, shards)}, device_id_type=MESH
            )
        h = h_ref[...].astype(F32)
        normed[...] = (
            h * lax.rsqrt(jnp.mean(h * h, -1, keepdims=True) + 1e-06) * g_ref[...]
        ).astype(BF16)
        sums[...] = jnp.zeros_like(sums)

    logits = jnp.dot(normed[...], w_ref[...], preferred_element_type=F32)
    lane = lax.broadcasted_iota(jnp.int32, (rows, 128), 1)
    marks = [t_ref[:, n : n + 1] for n in range(3)]
    new = [jnp.zeros((rows, 128), F32) for _ in range(4)]
    for b in range(tile // 128):
        col = step * tile + b * 128 + lane
        x = logits[:, b * 128 : (b + 1) * 128]
        new[0] += jnp.where(col < vocab, jnp.exp(x), 0.0)
        for n in range(3):
            new[n + 1] += jnp.where(col == marks[n], x, 0.0)
    for n in range(4):
        sums[n] += new[n]

    @pl.when(step == pl.num_programs(0) - 1)
    def _():
        stat = jnp.zeros((rows, 128), F32)
        for n in range(4):
            stat = jnp.where(lane == n, jnp.sum(sums[n], -1, keepdims=True), stat)
        stats[...] = jnp.transpose(stat)[:8]
        pl.semaphore_wait(barrier, shards - 1)

        def copy(k):
            return pltpu.make_async_remote_copy(
                src_ref=stats, dst_ref=slots.at[k], send_sem=send.at[k], recv_sem=recv.at[k],
                device_id={"mp": lax.rem(me + k, shards)}, device_id_type=MESH,
            )

        for k in range(1, shards):
            copy(k).start()
        total = stats[...]
        for k in range(1, shards):
            copy(k).wait_recv()
            total = total + slots[k]
        o_ref[...] = total
        for k in range(1, shards):
            copy(k).wait_send()


def score(shards, hidden, gain, marks, vocab_weight):
    rows, width = hidden.shape
    vocab = vocab_weight.shape[1]
    tile = 512
    dma = pltpu.SemaphoreType.DMA
    return pl.pallas_call(
        functools.partial(score_kernel, vocab, shards),
        grid=(pl.cdiv(vocab, tile),),
        in_specs=[
            pl.BlockSpec((rows, width), lambda i: (0, 0)),
            pl.BlockSpec((1, width), lambda i: (0, 0)),
            pl.BlockSpec((rows, 128), lambda i: (0, 0)),
            pl.BlockSpec((width, tile), lambda i: (0, i)),
        ],
        out_specs=pl.BlockSpec((8, rows), lambda i: (0, 0)),
        out_shape=jax.ShapeDtypeStruct((8, rows), F32),
        scratch_shapes=[
            pltpu.VMEM((rows, width), BF16),
            pltpu.VMEM((4, rows, 128), F32),
            pltpu.VMEM((8, rows), F32),
            pltpu.VMEM((shards, 8, rows), F32),
            dma((shards,)),
            dma((shards,)),
        ],
        compiler_params=pltpu.CompilerParams(
            collective_id=1, has_side_effects=True, vmem_limit_bytes=VMEM_LIMIT
        ),
        name="score_exchange",
    )(hidden, gain, marks, vocab_weight)


def local_fast(
    queries, new_keys, new_values, cache_keys, cache_values, lengths, parents, tree_tokens,
    residual, out_weight, norm_gain, vocab_weight,
):
    reqs, tree, width = queries.shape
    tokens = reqs * tree
    shard = lax.axis_index("mp")
    shards = lax.axis_size("mp")
    groups = lax.axis_size("dp")
    ncol = width // shards
    part = attention(
        shards, queries, new_keys, new_values, cache_keys, cache_values, lengths, parents
    ).reshape(shards, tokens // shards, width + 128)
    res = lax.dynamic_slice_in_dim(residual.reshape(tokens, width), shard * ncol, ncol, 1)
    res = res.reshape(shards, tokens // shards, ncol)
    hidden = hidden_of(shards, groups, part, out_weight, res).reshape(tokens, width)

    vocab = vocab_weight.shape[1]
    column = tree_tokens - shard * vocab
    column = jnp.where((column >= 0) & (column < vocab), column, -1)
    idx = jnp.arange(tree, dtype=jnp.int32)[None, :]
    by_one = (parents == idx - 1) & (idx > 0)
    by_two = (parents == idx - 2) & (idx > 1)

    def ahead(x, n):
        return jnp.pad(x[:, n:], ((0, 0), (0, n)), constant_values=-1)

    first = jnp.where(idx == 0, column, -1)
    marks = jnp.stack(
        [ahead(jnp.where(by_one, column, -1), 1), ahead(jnp.where(by_two, column, -1), 2), first], -1
    ).reshape(tokens, 3)
    marks = jnp.pad(marks, ((0, 0), (0, 125)), constant_values=-1)
    stats = score(shards, hidden, norm_gain.reshape(1, width), marks, vocab_weight)
    total = stats.reshape(8, reqs, tree)

    def behind(x, n):
        return jnp.pad(x[:, : tree - n], ((0, 0), (n, 0)))

    sums = total[0]
    picked = jnp.where(idx == 0, total[3], jnp.where(by_one, behind(total[1], 1), behind(total[2], 2)))
    norm = jnp.where(idx == 0, sums, jnp.where(by_one, behind(sums, 1), behind(sums, 2)))
    return (hidden.reshape(reqs, tree, width), picked - jnp.log(norm))


def local_plain(
    queries,
    new_keys,
    new_values,
    cache_keys,
    cache_values,
    lengths,
    parents,
    tree_tokens,
    residual,
    out_weight,
    norm_gain,
    vocab_weight,
):
    reqs, tree, width = queries.shape
    slots = cache_keys.shape[1]
    head_dim = width // HEADS
    scale = head_dim ** (-0.5)
    shard = lax.axis_index("mp")
    shards = lax.axis_size("mp")
    tokens = reqs * tree
    window = slots * shards // 2
    positions = shard * slots + jnp.arange(slots, dtype=jnp.int32)
    visible = (positions[None, :] < lengths[:, None]) & (
        (positions[None, :] < SINK) | (positions[None, :] >= lengths[:, None] - window)
    )
    q4 = queries.reshape(reqs, tree, HEADS, head_dim)
    k4 = cache_keys.reshape(reqs, slots, HEADS, head_dim)
    v4 = cache_values.reshape(reqs, slots, HEADS, head_dim)
    cache_e = jnp.where(
        visible[:, None, None, :],
        jnp.exp(jnp.einsum("rihd,rshd->rhis", q4, k4, preferred_element_type=jnp.float32) * scale),
        0.0,
    )
    cache_den = jnp.sum(cache_e, -1)
    cache_num = jnp.einsum(
        "rhis,rshd->rihd", cache_e.astype(jnp.bfloat16), v4, preferred_element_type=jnp.float32
    )
    ancestors = ancestor_mask(parents)
    nk4 = new_keys.reshape(reqs, tree, HEADS, head_dim)
    nv4 = new_values.reshape(reqs, tree, HEADS, head_dim)
    tree_e = jnp.where(
        ancestors[:, None],
        jnp.exp(jnp.einsum("rihd,rjhd->rhij", q4, nk4, preferred_element_type=jnp.float32) * scale),
        0.0,
    )
    tree_den = jnp.sum(tree_e, -1)
    tree_num = jnp.einsum(
        "rhij,rjhd->rihd", tree_e.astype(jnp.bfloat16), nv4, preferred_element_type=jnp.float32
    )
    flat_res = residual.reshape(tokens, width)
    num_all, den_all = lax.psum((cache_num.reshape(tokens, width), cache_den), "mp")
    denom = jnp.transpose(den_all + tree_den, (0, 2, 1))
    numer = num_all.reshape(reqs, tree, HEADS, head_dim) + tree_num
    attended = (numer / denom[..., None]).astype(jnp.bfloat16).reshape(tokens, width)
    projected = jnp.dot(
        attended,
        lax.all_gather(out_weight, ("dp", "mp"), axis=0, tiled=True),
        preferred_element_type=jnp.float32,
    )
    hidden = (flat_res.astype(jnp.float32) + projected).astype(jnp.bfloat16)
    hfloat = hidden.astype(jnp.float32)
    normed = (
        hfloat * lax.rsqrt(jnp.mean(hfloat * hfloat, -1, keepdims=True) + 1e-06) * norm_gain
    ).astype(jnp.bfloat16)
    vocab_dev = vocab_weight.shape[1]
    logits = jnp.dot(normed, vocab_weight, preferred_element_type=jnp.float32)
    exp_sums = jnp.sum(jnp.exp(logits), -1)
    parent_rows = (jnp.arange(reqs, dtype=jnp.int32)[:, None] * tree + parents).reshape(-1)
    column = tree_tokens.reshape(-1) - shard * vocab_dev
    inside = (column >= 0) & (column < vocab_dev)
    picked = jnp.where(inside, logits[parent_rows, jnp.clip(column, 0, vocab_dev - 1)], 0.0)
    parent_sums = exp_sums[parent_rows]
    total_sums, total_picked = lax.psum((parent_sums, picked), "mp")
    node_logprob = (total_picked - jnp.log(total_sums)).reshape(reqs, tree)
    return (hidden.reshape(reqs, tree, width), node_logprob)


def local(*args):
    queries, vocab_weight = args[0], args[-1]
    reqs, tree, width = queries.shape
    shards = lax.axis_size("mp")
    fits = (
        (reqs * tree) % (shards * 16) == 0
        and width % (shards * 128) == 0
        and width == HEADS * 128
        and tree % 16 == 0
        and shards % 2 == 0
        and shards >= 8
    )
    return (local_fast if fits else local_plain)(*args)


def solution(mesh):
    placed = (
        P("dp", None, None),
        P("dp", None, None),
        P("dp", None, None),
        P("dp", "mp", None),
        P("dp", "mp", None),
        P("dp"),
        P("dp", None),
        P("dp", None),
        P("dp", None, None),
        P(("dp", "mp"), None),
        P(),
        P(None, "mp"),
    )
    return jax.shard_map(
        local,
        mesh=mesh,
        in_specs=placed,
        out_specs=(P("dp", None, None), P("dp", None)),
        check_vma=False,
    )
```

```python
import functools

import jax
import jax.numpy as jnp
from jax import lax
from jax.experimental import pallas as pl
from jax.experimental.pallas import tpu as pltpu
from jax.sharding import PartitionSpec as P

HEADS = 16
SINK = 4
F32 = jnp.float32
BF16 = jnp.bfloat16
MESH = pl.DeviceIdType.MESH
VMEM_LIMIT = 60 * 1024 * 1024


def ancestor_mask(parents):
    tree = parents.shape[-1]
    idx = jnp.arange(tree, dtype=jnp.int32)
    links = (
        (idx[None, :, None] == idx[None, None, :]) | (parents[:, :, None] == idx[None, None, :])
    ).astype(F32)
    for _ in range((tree - 1).bit_length()):
        links = jnp.minimum(
            jnp.einsum("rij,rjk->rik", links, links, precision=lax.Precision.HIGHEST), 1.0
        )
    return links > 0.5


def attention_kernel(
    shards, len_ref, q_ref, k_ref, v_ref, nk_ref, nv_ref, par_ref, o_ref, chain
):
    req = pl.program_id(0)
    shard = lax.axis_index("mp")
    slots = k_ref.shape[1]
    tree, width = q_ref.shape[1:]
    reqs = par_ref.shape[0]
    hd = width // HEADS
    scale = hd ** (-0.5)
    cap = slots * shards
    length = len_ref[req]
    start = shard * slots
    tree_shard = max(shards // 8, 1)
    seen = (start < length) & ((start < SINK) | (start + slots > length - cap // 2))

    def attend(keys, values, mask):
        lane = lax.broadcasted_iota(jnp.int32, (tree, 128), 1)
        low = lax.broadcasted_iota(jnp.int32, (tree, 2 * hd), 1) < hd
        mask2 = jnp.concatenate([mask, mask], 0)
        den = jnp.zeros((tree, 128), F32)
        pairs = HEADS // 2
        for group in range(0, pairs, 4):
            scores = []
            for p in range(group, group + 4):
                cols = slice(2 * p * hd, 2 * (p + 1) * hd)
                q = q_ref[0, :, cols]
                both = jnp.concatenate(
                    [jnp.where(low, q, jnp.zeros_like(q)), jnp.where(low, jnp.zeros_like(q), q)], 0
                )
                scores.append(
                    lax.dot_general(
                        both, keys[0, :, cols], (((1,), (1,)), ((), ())),
                        preferred_element_type=F32,
                    )
                )
            es = [jnp.where(mask2 > 0.5, jnp.exp(s * scale), 0.0) for s in scores]
            for n, e in enumerate(es):
                p = group + n
                cols = slice(2 * p * hd, 2 * (p + 1) * hd)
                num = jnp.dot(e.astype(BF16), values[0, :, cols], preferred_element_type=F32)
                o_ref[0, :, 2 * p * hd : (2 * p + 1) * hd] = num[:tree, :hd].astype(BF16)
                o_ref[0, :, (2 * p + 1) * hd : 2 * (p + 1) * hd] = num[tree:, hd:].astype(BF16)
                d = jnp.sum(e, -1, keepdims=True)
                den = jnp.where(lane == 2 * p, d[:tree], den)
                den = jnp.where(lane == 2 * p + 1, d[tree:], den)
        o_ref[0, :, width:] = den.astype(BF16)

    @pl.when((shard == tree_shard) & (req == 0))
    def _():
        node = lax.broadcasted_iota(jnp.int32, (reqs, 128), 1)
        rows = []
        for j in range(tree):
            row = jnp.where(node == j, 1.0, 0.0)
            if j == 1:
                row = row + rows[0]
            elif j > 1:
                row = row + jnp.where(par_ref[:, j : j + 1] == j - 1, rows[j - 1], rows[j - 2])
            rows.append(row)
            chain[j] = row

    @pl.when(shard == tree_shard)
    def _():
        attend(nk_ref, nv_ref, chain[:, req, :][:, :tree])

    @pl.when((shard != tree_shard) & seen)
    def _():
        pos = start + lax.broadcasted_iota(jnp.int32, (tree, slots), 1)
        mask = (pos < length) & ((pos < SINK) | (pos >= length - cap // 2))
        attend(k_ref, v_ref, jnp.where(mask, 1.0, 0.0))

    @pl.when((shard != tree_shard) & jnp.logical_not(seen))
    def _():
        o_ref[...] = jnp.zeros_like(o_ref)


def attention(shards, queries, new_keys, new_values, cache_keys, cache_values, lengths, parents):
    reqs, tree, width = queries.shape
    slots = cache_keys.shape[1]

    def block(rows, cols):
        return pl.BlockSpec((1, rows, cols), lambda r: (r, 0, 0))

    return pl.pallas_call(
        functools.partial(attention_kernel, shards),
        grid=(reqs,),
        in_specs=[
            pl.BlockSpec(memory_space=pltpu.SMEM),
            block(tree, width),
            block(slots, width),
            block(slots, width),
            block(tree, width),
            block(tree, width),
            pl.BlockSpec((reqs, tree), lambda r: (0, 0)),
        ],
        out_specs=block(tree, width + 128),
        out_shape=jax.ShapeDtypeStruct((reqs, tree, width + 128), BF16),
        scratch_shapes=[pltpu.VMEM((tree, reqs, 128), F32)],
        compiler_params=pltpu.CompilerParams(vmem_limit_bytes=VMEM_LIMIT),
        name="attention_part",
    )(lengths, queries, cache_keys, cache_values, new_keys, new_values, parents)


def when(cond, fn):
    pl.when(cond)(fn)


class Line:
    def __init__(self, chips, at, recv, send_r, send_l, send_s):
        me = lax.axis_index("mp")
        self.chips, self.at, self.recv = chips, at, recv
        self.sends = send_r, send_l, send_s
        self.me, self.c, self.z = me, lax.rem(me, 2), lax.div(me, 2)
        self.sib = 2 * self.z + 1 - self.c

    def copy(self, slot, sem, to):
        return pltpu.make_async_remote_copy(
            src_ref=self.at(slot), dst_ref=self.at(slot), send_sem=sem,
            recv_sem=self.recv.at[slot], device_id={"mp": to}, device_id_type=MESH,
        )

    def right(self, k):
        return self.copy(2 * (self.z - k) + self.c, self.sends[0].at[k], self.me + 2)

    def left(self, k):
        return self.copy(2 * (self.z + k) + self.c, self.sends[1].at[k], self.me - 2)

    def pair(self, zs):
        return self.copy(2 * zs + self.c, self.sends[2].at[zs], self.sib)

    def start(self):
        when(self.z < self.chips - 1, lambda: self.right(0).start())
        when(self.z > 0, lambda: self.left(0).start())
        self.pair(self.z).start()

    def forward(self, k):
        z, chips = self.z, self.chips

        @pl.when(z - k >= 0)
        def _():
            self.right(k).wait_recv()
            when(z < chips - 1, lambda: self.right(k).start())
            self.pair(z - k).start()

        @pl.when(z + k <= chips - 1)
        def _():
            self.left(k).wait_recv()
            when(z > 0, lambda: self.left(k).start())
            self.pair(z + k).start()

    def arrive(self):
        for zs in range(self.chips):
            self.copy(2 * zs + 1 - self.c, self.sends[2].at[zs], self.sib).wait_recv()

    def finish(self):
        z, chips = self.z, self.chips
        for k in range(chips):
            when((z - k >= 0) & (z < chips - 1), lambda: self.right(k).wait_send())
            when((z + k <= chips - 1) & (z > 0), lambda: self.left(k).wait_send())
        for zs in range(chips):
            self.pair(zs).wait_send()


CHUNK = 16


def hidden_kernel(
    chips, groups, part, w_ref, res_ref, out_ref,
    own_buf, sib_buf, from_l, from_r, acc, tot, att, wcol, hcol,
    own_s, sib_s, sib_r, fl_r, fr_r, acc_s, g1_r, g1_a, g1_b, g1_c, g2_r, g2_a, g2_b, g2_c,
    w1_s, w1_r, w2_s, w2_r, wown_s,
):
    shards = 2 * chips
    me = lax.axis_index("mp")
    grp = lax.axis_index("dp")
    c, z = lax.rem(me, 2), lax.div(me, 2)
    sib = 2 * z + 1 - c
    width = att.shape[-1]
    hd = width // HEADS
    ncol = wcol.shape[-1]
    chunks = att.shape[1] // CHUNK

    def rows(i):
        return pl.ds(i * CHUNK, CHUNK)

    def columns(j):
        return pl.ds(pl.multiple_of(j * ncol, 128), ncol)

    barrier = pltpu.get_barrier_semaphore()
    for k in range(1, shards):
        pl.semaphore_signal(
            barrier, inc=1, device_id={"mp": lax.rem(me + k, shards)}, device_id_type=MESH
        )
    for k in range(1, groups):
        pl.semaphore_signal(
            barrier, inc=1, device_id={"dp": lax.rem(grp + k, groups)}, device_id_type=MESH
        )

    order = []
    for k in range(chips):
        for zd in (chips - 1 - k, k):
            if zd not in order:
                order.append(zd)

    def mine(i, zd):
        return pltpu.make_async_copy(
            part.at[2 * zd + c, rows(i)], own_buf.at[zd, rows(i)], own_s.at[i, zd]
        )

    for i in range(chunks):
        for zd in order:
            mine(i, zd).start()
    own_w = pltpu.make_async_copy(w_ref.at[:, columns(me)], wcol.at[grp, me], wown_s)
    own_w.start()

    pl.semaphore_wait(barrier, shards - 1 + groups - 1)

    def pair(i, zd):
        return pltpu.make_async_remote_copy(
            src_ref=part.at[2 * zd + 1 - c, rows(i)], dst_ref=sib_buf.at[zd, rows(i)],
            send_sem=sib_s.at[i, zd], recv_sem=sib_r.at[i, zd],
            device_id={"mp": sib}, device_id_type=MESH,
        )

    for i in range(chunks):
        for zd in order:
            pair(i, zd).start()

    def w_mp(k):
        to = lax.rem(me + k, shards)
        return pltpu.make_async_remote_copy(
            src_ref=w_ref.at[:, columns(to)], dst_ref=wcol.at[grp, me], send_sem=w1_s.at[k],
            recv_sem=w1_r.at[k], device_id={"mp": to}, device_id_type=MESH,
        )

    def w_dp(k, src):
        return pltpu.make_async_remote_copy(
            src_ref=wcol.at[src], dst_ref=wcol.at[src], send_sem=w2_s.at[k],
            recv_sem=w2_r.at[k], device_id={"dp": lax.rem(grp + k, groups)}, device_id_type=MESH,
        )

    def pass_on(i, zd, buf, sems, to):
        return pltpu.make_async_remote_copy(
            src_ref=acc.at[zd, rows(i)], dst_ref=buf.at[zd, rows(i)], send_sem=acc_s.at[i, zd],
            recv_sem=sems.at[i, zd], device_id={"mp": to}, device_id_type=MESH,
        )

    def both(i, zd):
        return own_buf[zd, rows(i)].astype(F32) + sib_buf[zd, rows(i)].astype(F32)

    def arrive(i, zd):
        mine(i, zd).wait()
        pair(i, zd).wait_recv()

    def step(i, zd, buf, sems, first, to):
        arrive(i, zd)

        @pl.when(first)
        def _():
            acc[zd, rows(i)] = both(i, zd).astype(BF16)

        @pl.when(jnp.logical_not(first))
        def _():
            pass_on(i, zd, buf, sems, to).wait_recv()
            acc[zd, rows(i)] = (both(i, zd) + buf[zd, rows(i)].astype(F32)).astype(BF16)

        pass_on(i, zd, buf, sems, to).start()

    def sums(i, k):
        rd, ld = chips - 1 - k, k
        when(rd > z, functools.partial(step, i, rd, from_l, fl_r, z == 0, me + 2))
        when(ld < z, functools.partial(step, i, ld, from_r, fr_r, z == chips - 1, me - 2))

    first = [
        Line(chips, lambda j, i=i: att.at[j, rows(i)], g1_r.at[i], g1_a.at[i], g1_b.at[i], g1_c.at[i])
        for i in range(chunks)
    ]
    second = [
        Line(chips, lambda j, i=i: hcol.at[j, i], g2_r.at[i], g2_a.at[i], g2_b.at[i], g2_c.at[i])
        for i in range(chunks)
    ]

    def attended(i):
        arrive(i, z)
        tot[...] = both(i, z)

        @pl.when(z > 0)
        def _():
            pass_on(i, z, from_l, fl_r, me).wait_recv()
            tot[...] += from_l[z, rows(i)].astype(F32)

        @pl.when(z < chips - 1)
        def _():
            pass_on(i, z, from_r, fr_r, me).wait_recv()
            tot[...] += from_r[z, rows(i)].astype(F32)

        for h in range(HEADS):
            cols = slice(h * hd, (h + 1) * hd)
            att[me, rows(i), cols] = (tot[:, cols] / tot[:, width + h : width + h + 1]).astype(BF16)
        first[i].start()

    def project(i):
        first[i].arrive()
        if i == 0:
            for k in range(1, groups):
                w_dp(k, lax.rem(grp + groups - k, groups)).wait_recv()
        projected = jnp.dot(
            att[:, rows(i), :].reshape(shards * CHUNK, width),
            wcol[...].reshape(width, ncol),
            preferred_element_type=F32,
        )
        res = res_ref[:, rows(i), :].reshape(shards * CHUNK, ncol)
        hcol[me, i] = (res.astype(F32) + projected).astype(BF16)
        second[i].start()

    def place(i):
        second[i].arrive()
        for j in range(shards):
            for t in range(shards):
                out_ref[t, rows(i), j * ncol : (j + 1) * ncol] = hcol[
                    j, i, t * CHUNK : (t + 1) * CHUNK
                ]

    for k in range(chips - 1):
        for i in range(chunks):
            sums(i, k)
        if k == 0:
            for n in range(1, shards):
                w_mp(n).start()
    for i in range(chunks):
        attended(i)
    for n in range(1, shards):
        w_mp(n).wait_recv()
    own_w.wait()
    for n in range(1, groups):
        w_dp(n, grp).start()
    for k in range(1, chips):
        for i in range(chunks):
            first[i].forward(k)
    for i in range(chunks):
        project(i)
    for k in range(1, chips):
        for i in range(chunks):
            second[i].forward(k)
    for i in range(chunks):
        place(i)

    for i in range(chunks):
        first[i].finish()
        second[i].finish()
        for zd in range(chips):
            pair(i, zd).wait_send()
            when(zd != z, lambda: pass_on(i, zd, from_l, fl_r, me).wait_send())
    for k in range(1, shards):
        w_mp(k).wait_send()
    for k in range(1, groups):
        w_dp(k, grp).wait_send()


def hidden_of(shards, groups, part, out_weight, res):
    own, width = part.shape[1], out_weight.shape[1]
    wide = part.shape[2]
    ncol = width // shards
    chips = shards // 2
    chunks = own // CHUNK
    dma = pltpu.SemaphoreType.DMA
    gather_sems = [dma((chunks, shards))] + [dma((chunks, chips))] * 3
    vmem = pl.BlockSpec(memory_space=pltpu.VMEM)
    return pl.pallas_call(
        functools.partial(hidden_kernel, chips, groups),
        in_specs=[pl.BlockSpec(memory_space=pl.ANY), vmem, vmem],
        out_specs=vmem,
        out_shape=jax.ShapeDtypeStruct((shards, own, width), BF16),
        scratch_shapes=[
            pltpu.VMEM((chips, own, wide), BF16),
            pltpu.VMEM((chips, own, wide), BF16),
            pltpu.VMEM((chips, own, wide), BF16),
            pltpu.VMEM((chips, own, wide), BF16),
            pltpu.VMEM((chips, own, wide), BF16),
            pltpu.VMEM((CHUNK, wide), F32),
            pltpu.VMEM((shards, own, width), BF16),
            pltpu.VMEM((groups, shards, out_weight.shape[0], ncol), BF16),
            pltpu.VMEM((shards, chunks, shards * CHUNK, ncol), BF16),
            *[dma((chunks, chips))] * 6,
            *gather_sems,
            *gather_sems,
            dma((shards,)), dma((shards,)), dma((groups,)), dma((groups,)), dma,
        ],
        compiler_params=pltpu.CompilerParams(
            collective_id=0, has_side_effects=True, vmem_limit_bytes=VMEM_LIMIT
        ),
        name="hidden_exchange",
    )(part, out_weight, res)


def score_kernel(vocab, shards, h_ref, g_ref, t_ref, w_ref, o_ref, normed, sums, stats, slots, send, recv):
    step = pl.program_id(0)
    tile = w_ref.shape[1]
    rows = h_ref.shape[0]
    me = lax.axis_index("mp")
    barrier = pltpu.get_barrier_semaphore()

    @pl.when(step == 0)
    def _():
        for k in range(1, shards):
            pl.semaphore_signal(
                barrier, inc=1, device_id={"mp": lax.rem(me + k, shards)}, device_id_type=MESH
            )
        h = h_ref[...].astype(F32)
        normed[...] = (
            h * lax.rsqrt(jnp.mean(h * h, -1, keepdims=True) + 1e-06) * g_ref[...]
        ).astype(BF16)
        sums[...] = jnp.zeros_like(sums)

    logits = jnp.dot(normed[...], w_ref[...], preferred_element_type=F32)
    lane = lax.broadcasted_iota(jnp.int32, (rows, 128), 1)
    marks = [t_ref[:, n : n + 1] for n in range(3)]
    new = [jnp.zeros((rows, 128), F32) for _ in range(4)]
    for b in range(tile // 128):
        col = step * tile + b * 128 + lane
        x = logits[:, b * 128 : (b + 1) * 128]
        new[0] += jnp.where(col < vocab, jnp.exp(x), 0.0)
        for n in range(3):
            new[n + 1] += jnp.where(col == marks[n], x, 0.0)
    for n in range(4):
        sums[n] += new[n]

    @pl.when(step == pl.num_programs(0) - 1)
    def _():
        stat = jnp.zeros((rows, 128), F32)
        for n in range(4):
            stat = jnp.where(lane == n, jnp.sum(sums[n], -1, keepdims=True), stat)
        stats[...] = jnp.transpose(stat)[:8]
        pl.semaphore_wait(barrier, shards - 1)

        def copy(k):
            return pltpu.make_async_remote_copy(
                src_ref=stats, dst_ref=slots.at[k], send_sem=send.at[k], recv_sem=recv.at[k],
                device_id={"mp": lax.rem(me + k, shards)}, device_id_type=MESH,
            )

        for k in range(1, shards):
            copy(k).start()
        total = stats[...]
        for k in range(1, shards):
            copy(k).wait_recv()
            total = total + slots[k]
        o_ref[...] = total
        for k in range(1, shards):
            copy(k).wait_send()


def score(shards, hidden, gain, marks, vocab_weight):
    rows, width = hidden.shape
    vocab = vocab_weight.shape[1]
    tile = 512
    dma = pltpu.SemaphoreType.DMA
    return pl.pallas_call(
        functools.partial(score_kernel, vocab, shards),
        grid=(pl.cdiv(vocab, tile),),
        in_specs=[
            pl.BlockSpec((rows, width), lambda i: (0, 0)),
            pl.BlockSpec((1, width), lambda i: (0, 0)),
            pl.BlockSpec((rows, 128), lambda i: (0, 0)),
            pl.BlockSpec((width, tile), lambda i: (0, i)),
        ],
        out_specs=pl.BlockSpec((8, rows), lambda i: (0, 0)),
        out_shape=jax.ShapeDtypeStruct((8, rows), F32),
        scratch_shapes=[
            pltpu.VMEM((rows, width), BF16),
            pltpu.VMEM((4, rows, 128), F32),
            pltpu.VMEM((8, rows), F32),
            pltpu.VMEM((shards, 8, rows), F32),
            dma((shards,)),
            dma((shards,)),
        ],
        compiler_params=pltpu.CompilerParams(
            collective_id=1, has_side_effects=True, vmem_limit_bytes=VMEM_LIMIT
        ),
        name="score_exchange",
    )(hidden, gain, marks, vocab_weight)


def local_fast(
    queries, new_keys, new_values, cache_keys, cache_values, lengths, parents, tree_tokens,
    residual, out_weight, norm_gain, vocab_weight,
):
    reqs, tree, width = queries.shape
    tokens = reqs * tree
    shard = lax.axis_index("mp")
    shards = lax.axis_size("mp")
    groups = lax.axis_size("dp")
    ncol = width // shards
    part = attention(
        shards, queries, new_keys, new_values, cache_keys, cache_values, lengths, parents
    ).reshape(shards, tokens // shards, width + 128)
    res = lax.dynamic_slice_in_dim(residual.reshape(tokens, width), shard * ncol, ncol, 1)
    res = res.reshape(shards, tokens // shards, ncol)
    hidden = hidden_of(shards, groups, part, out_weight, res).reshape(tokens, width)

    vocab = vocab_weight.shape[1]
    column = tree_tokens - shard * vocab
    column = jnp.where((column >= 0) & (column < vocab), column, -1)
    idx = jnp.arange(tree, dtype=jnp.int32)[None, :]
    by_one = (parents == idx - 1) & (idx > 0)
    by_two = (parents == idx - 2) & (idx > 1)

    def ahead(x, n):
        return jnp.pad(x[:, n:], ((0, 0), (0, n)), constant_values=-1)

    first = jnp.where(idx == 0, column, -1)
    marks = jnp.stack(
        [ahead(jnp.where(by_one, column, -1), 1), ahead(jnp.where(by_two, column, -1), 2), first], -1
    ).reshape(tokens, 3)
    marks = jnp.pad(marks, ((0, 0), (0, 125)), constant_values=-1)
    stats = score(shards, hidden, norm_gain.reshape(1, width), marks, vocab_weight)
    total = stats.reshape(8, reqs, tree)

    def behind(x, n):
        return jnp.pad(x[:, : tree - n], ((0, 0), (n, 0)))

    sums = total[0]
    picked = jnp.where(idx == 0, total[3], jnp.where(by_one, behind(total[1], 1), behind(total[2], 2)))
    norm = jnp.where(idx == 0, sums, jnp.where(by_one, behind(sums, 1), behind(sums, 2)))
    return (hidden.reshape(reqs, tree, width), picked - jnp.log(norm))


def local_plain(
    queries,
    new_keys,
    new_values,
    cache_keys,
    cache_values,
    lengths,
    parents,
    tree_tokens,
    residual,
    out_weight,
    norm_gain,
    vocab_weight,
):
    reqs, tree, width = queries.shape
    slots = cache_keys.shape[1]
    head_dim = width // HEADS
    scale = head_dim ** (-0.5)
    shard = lax.axis_index("mp")
    shards = lax.axis_size("mp")
    tokens = reqs * tree
    window = slots * shards // 2
    positions = shard * slots + jnp.arange(slots, dtype=jnp.int32)
    visible = (positions[None, :] < lengths[:, None]) & (
        (positions[None, :] < SINK) | (positions[None, :] >= lengths[:, None] - window)
    )
    q4 = queries.reshape(reqs, tree, HEADS, head_dim)
    k4 = cache_keys.reshape(reqs, slots, HEADS, head_dim)
    v4 = cache_values.reshape(reqs, slots, HEADS, head_dim)
    cache_e = jnp.where(
        visible[:, None, None, :],
        jnp.exp(jnp.einsum("rihd,rshd->rhis", q4, k4, preferred_element_type=jnp.float32) * scale),
        0.0,
    )
    cache_den = jnp.sum(cache_e, -1)
    cache_num = jnp.einsum(
        "rhis,rshd->rihd", cache_e.astype(jnp.bfloat16), v4, preferred_element_type=jnp.float32
    )
    ancestors = ancestor_mask(parents)
    nk4 = new_keys.reshape(reqs, tree, HEADS, head_dim)
    nv4 = new_values.reshape(reqs, tree, HEADS, head_dim)
    tree_e = jnp.where(
        ancestors[:, None],
        jnp.exp(jnp.einsum("rihd,rjhd->rhij", q4, nk4, preferred_element_type=jnp.float32) * scale),
        0.0,
    )
    tree_den = jnp.sum(tree_e, -1)
    tree_num = jnp.einsum(
        "rhij,rjhd->rihd", tree_e.astype(jnp.bfloat16), nv4, preferred_element_type=jnp.float32
    )
    flat_res = residual.reshape(tokens, width)
    num_all, den_all = lax.psum((cache_num.reshape(tokens, width), cache_den), "mp")
    denom = jnp.transpose(den_all + tree_den, (0, 2, 1))
    numer = num_all.reshape(reqs, tree, HEADS, head_dim) + tree_num
    attended = (numer / denom[..., None]).astype(jnp.bfloat16).reshape(tokens, width)
    projected = jnp.dot(
        attended,
        lax.all_gather(out_weight, ("dp", "mp"), axis=0, tiled=True),
        preferred_element_type=jnp.float32,
    )
    hidden = (flat_res.astype(jnp.float32) + projected).astype(jnp.bfloat16)
    hfloat = hidden.astype(jnp.float32)
    normed = (
        hfloat * lax.rsqrt(jnp.mean(hfloat * hfloat, -1, keepdims=True) + 1e-06) * norm_gain
    ).astype(jnp.bfloat16)
    vocab_dev = vocab_weight.shape[1]
    logits = jnp.dot(normed, vocab_weight, preferred_element_type=jnp.float32)
    exp_sums = jnp.sum(jnp.exp(logits), -1)
    parent_rows = (jnp.arange(reqs, dtype=jnp.int32)[:, None] * tree + parents).reshape(-1)
    column = tree_tokens.reshape(-1) - shard * vocab_dev
    inside = (column >= 0) & (column < vocab_dev)
    picked = jnp.where(inside, logits[parent_rows, jnp.clip(column, 0, vocab_dev - 1)], 0.0)
    parent_sums = exp_sums[parent_rows]
    total_sums, total_picked = lax.psum((parent_sums, picked), "mp")
    node_logprob = (total_picked - jnp.log(total_sums)).reshape(reqs, tree)
    return (hidden.reshape(reqs, tree, width), node_logprob)


def local(*args):
    queries, vocab_weight = args[0], args[-1]
    reqs, tree, width = queries.shape
    shards = lax.axis_size("mp")
    fits = (
        (reqs * tree) % (shards * 16) == 0
        and width % (shards * 128) == 0
        and width == HEADS * 128
        and tree % 16 == 0
        and shards % 2 == 0
        and shards >= 8
    )
    return (local_fast if fits else local_plain)(*args)


def solution(mesh):
    placed = (
        P("dp", None, None),
        P("dp", None, None),
        P("dp", None, None),
        P("dp", "mp", None),
        P("dp", "mp", None),
        P("dp"),
        P("dp", None),
        P("dp", None),
        P("dp", None, None),
        P(("dp", "mp"), None),
        P(),
        P(None, "mp"),
    )
    return jax.shard_map(
        local,
        mesh=mesh,
        in_specs=placed,
        out_specs=(P("dp", None, None), P("dp", None)),
        check_vma=False,
    )
```

```python
import functools

import jax
import jax.numpy as jnp
from jax import lax
from jax.experimental import pallas as pl
from jax.experimental.pallas import tpu as pltpu
from jax.sharding import PartitionSpec as P

HEADS = 16
SINK = 4
F32 = jnp.float32
BF16 = jnp.bfloat16
MESH = pl.DeviceIdType.MESH
VMEM_LIMIT = 60 * 1024 * 1024


def ancestor_mask(parents):
    tree = parents.shape[-1]
    idx = jnp.arange(tree, dtype=jnp.int32)
    links = (
        (idx[None, :, None] == idx[None, None, :]) | (parents[:, :, None] == idx[None, None, :])
    ).astype(F32)
    for _ in range((tree - 1).bit_length()):
        links = jnp.minimum(
            jnp.einsum("rij,rjk->rik", links, links, precision=lax.Precision.HIGHEST), 1.0
        )
    return links > 0.5


def attention_kernel(
    shards, len_ref, q_ref, k_ref, v_ref, nk_ref, nv_ref, par_ref, o_ref, chain
):
    req = pl.program_id(0)
    shard = lax.axis_index("mp")
    slots = k_ref.shape[1]
    tree, width = q_ref.shape[1:]
    reqs = par_ref.shape[0]
    hd = width // HEADS
    scale = hd ** (-0.5)
    cap = slots * shards
    length = len_ref[req]
    start = shard * slots
    tree_shard = max(shards // 8, 1)
    seen = (start < length) & ((start < SINK) | (start + slots > length - cap // 2))

    def attend(keys, values, mask):
        lane = lax.broadcasted_iota(jnp.int32, (tree, 128), 1)
        low = lax.broadcasted_iota(jnp.int32, (tree, 2 * hd), 1) < hd
        mask2 = jnp.concatenate([mask, mask], 0)
        den = jnp.zeros((tree, 128), F32)
        pairs = HEADS // 2
        for group in range(0, pairs, 4):
            scores = []
            for p in range(group, group + 4):
                cols = slice(2 * p * hd, 2 * (p + 1) * hd)
                q = q_ref[0, :, cols]
                both = jnp.concatenate(
                    [jnp.where(low, q, jnp.zeros_like(q)), jnp.where(low, jnp.zeros_like(q), q)], 0
                )
                scores.append(
                    lax.dot_general(
                        both, keys[0, :, cols], (((1,), (1,)), ((), ())),
                        preferred_element_type=F32,
                    )
                )
            es = [jnp.where(mask2 > 0.5, jnp.exp(s * scale), 0.0) for s in scores]
            for n, e in enumerate(es):
                p = group + n
                cols = slice(2 * p * hd, 2 * (p + 1) * hd)
                num = jnp.dot(e.astype(BF16), values[0, :, cols], preferred_element_type=F32)
                o_ref[0, :, 2 * p * hd : (2 * p + 1) * hd] = num[:tree, :hd].astype(BF16)
                o_ref[0, :, (2 * p + 1) * hd : 2 * (p + 1) * hd] = num[tree:, hd:].astype(BF16)
                d = jnp.sum(e, -1, keepdims=True)
                den = jnp.where(lane == 2 * p, d[:tree], den)
                den = jnp.where(lane == 2 * p + 1, d[tree:], den)
        o_ref[0, :, width:] = den.astype(BF16)

    @pl.when((shard == tree_shard) & (req == 0))
    def _():
        node = lax.broadcasted_iota(jnp.int32, (reqs, 128), 1)
        rows = []
        for j in range(tree):
            row = jnp.where(node == j, 1.0, 0.0)
            if j == 1:
                row = row + rows[0]
            elif j > 1:
                row = row + jnp.where(par_ref[:, j : j + 1] == j - 1, rows[j - 1], rows[j - 2])
            rows.append(row)
            chain[j] = row

    @pl.when(shard == tree_shard)
    def _():
        attend(nk_ref, nv_ref, chain[:, req, :][:, :tree])

    @pl.when((shard != tree_shard) & seen)
    def _():
        pos = start + lax.broadcasted_iota(jnp.int32, (tree, slots), 1)
        mask = (pos < length) & ((pos < SINK) | (pos >= length - cap // 2))
        attend(k_ref, v_ref, jnp.where(mask, 1.0, 0.0))

    @pl.when((shard != tree_shard) & jnp.logical_not(seen))
    def _():
        o_ref[...] = jnp.zeros_like(o_ref)


def attention(shards, queries, new_keys, new_values, cache_keys, cache_values, lengths, parents):
    reqs, tree, width = queries.shape
    slots = cache_keys.shape[1]

    def block(rows, cols):
        return pl.BlockSpec((1, rows, cols), lambda r: (r, 0, 0))

    return pl.pallas_call(
        functools.partial(attention_kernel, shards),
        grid=(reqs,),
        in_specs=[
            pl.BlockSpec(memory_space=pltpu.SMEM),
            block(tree, width),
            block(slots, width),
            block(slots, width),
            block(tree, width),
            block(tree, width),
            pl.BlockSpec((reqs, tree), lambda r: (0, 0)),
        ],
        out_specs=block(tree, width + 128),
        out_shape=jax.ShapeDtypeStruct((reqs, tree, width + 128), BF16),
        scratch_shapes=[pltpu.VMEM((tree, reqs, 128), F32)],
        compiler_params=pltpu.CompilerParams(vmem_limit_bytes=VMEM_LIMIT),
        name="attention_part",
    )(lengths, queries, cache_keys, cache_values, new_keys, new_values, parents)


def when(cond, fn):
    pl.when(cond)(fn)


class Line:
    def __init__(self, chips, at, recv, send_r, send_l, send_s):
        me = lax.axis_index("mp")
        self.chips, self.at, self.recv = chips, at, recv
        self.sends = send_r, send_l, send_s
        self.me, self.c, self.z = me, lax.rem(me, 2), lax.div(me, 2)
        self.sib = 2 * self.z + 1 - self.c

    def copy(self, slot, sem, to):
        return pltpu.make_async_remote_copy(
            src_ref=self.at(slot), dst_ref=self.at(slot), send_sem=sem,
            recv_sem=self.recv.at[slot], device_id={"mp": to}, device_id_type=MESH,
        )

    def right(self, k):
        return self.copy(2 * (self.z - k) + self.c, self.sends[0].at[k], self.me + 2)

    def left(self, k):
        return self.copy(2 * (self.z + k) + self.c, self.sends[1].at[k], self.me - 2)

    def pair(self, zs):
        return self.copy(2 * zs + self.c, self.sends[2].at[zs], self.sib)

    def start(self):
        when(self.z < self.chips - 1, lambda: self.right(0).start())
        when(self.z > 0, lambda: self.left(0).start())
        self.pair(self.z).start()

    def forward(self, k):
        z, chips = self.z, self.chips

        @pl.when(z - k >= 0)
        def _():
            self.right(k).wait_recv()
            when(z < chips - 1, lambda: self.right(k).start())
            self.pair(z - k).start()

        @pl.when(z + k <= chips - 1)
        def _():
            self.left(k).wait_recv()
            when(z > 0, lambda: self.left(k).start())
            self.pair(z + k).start()

    def arrive(self):
        for zs in range(self.chips):
            self.copy(2 * zs + 1 - self.c, self.sends[2].at[zs], self.sib).wait_recv()

    def finish(self):
        z, chips = self.z, self.chips
        for k in range(chips):
            when((z - k >= 0) & (z < chips - 1), lambda: self.right(k).wait_send())
            when((z + k <= chips - 1) & (z > 0), lambda: self.left(k).wait_send())
        for zs in range(chips):
            self.pair(zs).wait_send()


CHUNK = 16


def hidden_kernel(
    chips, groups, part, w_ref, res_ref, gain_ref, mark_ref, vocab_ref, out_ref, stat_ref,
    own_buf, sib_buf, from_l, from_r, acc, tot, att, wcol, hcol,
    own_s, sib_s, sib_r, fl_r, fr_r, acc_s, g1_r, g1_a, g1_b, g1_c, g2_r, g2_a, g2_b, g2_c,
    w1_s, w1_r, w2_s, w2_r, wown_s, vbuf, stats, slots, t_s, t_r, v_s,
):
    shards = 2 * chips
    me = lax.axis_index("mp")
    grp = lax.axis_index("dp")
    c, z = lax.rem(me, 2), lax.div(me, 2)
    sib = 2 * z + 1 - c
    width = att.shape[-1]
    hd = width // HEADS
    ncol = wcol.shape[-1]
    chunks = att.shape[1] // CHUNK

    def rows(i):
        return pl.ds(i * CHUNK, CHUNK)

    def columns(j):
        return pl.ds(pl.multiple_of(j * ncol, 128), ncol)

    barrier = pltpu.get_barrier_semaphore()
    for k in range(1, shards):
        pl.semaphore_signal(
            barrier, inc=1, device_id={"mp": lax.rem(me + k, shards)}, device_id_type=MESH
        )
    for k in range(1, groups):
        pl.semaphore_signal(
            barrier, inc=1, device_id={"dp": lax.rem(grp + k, groups)}, device_id_type=MESH
        )

    order = []
    for k in range(chips):
        for zd in (chips - 1 - k, k):
            if zd not in order:
                order.append(zd)

    def mine(i, zd):
        return pltpu.make_async_copy(
            part.at[2 * zd + c, rows(i)], own_buf.at[zd, rows(i)], own_s.at[i, zd]
        )

    for i in range(chunks):
        for zd in order:
            mine(i, zd).start()
    own_w = pltpu.make_async_copy(w_ref.at[:, columns(me)], wcol.at[grp, me], wown_s)
    own_w.start()
    load_vocab = pltpu.make_async_copy(vocab_ref, vbuf, v_s)
    load_vocab.start()

    pl.semaphore_wait(barrier, shards - 1 + groups - 1)

    def pair(i, zd):
        return pltpu.make_async_remote_copy(
            src_ref=part.at[2 * zd + 1 - c, rows(i)], dst_ref=sib_buf.at[zd, rows(i)],
            send_sem=sib_s.at[i, zd], recv_sem=sib_r.at[i, zd],
            device_id={"mp": sib}, device_id_type=MESH,
        )

    for i in range(chunks):
        for zd in order:
            pair(i, zd).start()

    def w_mp(k):
        to = lax.rem(me + k, shards)
        return pltpu.make_async_remote_copy(
            src_ref=w_ref.at[:, columns(to)], dst_ref=wcol.at[grp, me], send_sem=w1_s.at[k],
            recv_sem=w1_r.at[k], device_id={"mp": to}, device_id_type=MESH,
        )

    def w_dp(k, src):
        return pltpu.make_async_remote_copy(
            src_ref=wcol.at[src], dst_ref=wcol.at[src], send_sem=w2_s.at[k],
            recv_sem=w2_r.at[k], device_id={"dp": lax.rem(grp + k, groups)}, device_id_type=MESH,
        )

    def pass_on(i, zd, buf, sems, to):
        return pltpu.make_async_remote_copy(
            src_ref=acc.at[zd, rows(i)], dst_ref=buf.at[zd, rows(i)], send_sem=acc_s.at[i, zd],
            recv_sem=sems.at[i, zd], device_id={"mp": to}, device_id_type=MESH,
        )

    def both(i, zd):
        return own_buf[zd, rows(i)].astype(F32) + sib_buf[zd, rows(i)].astype(F32)

    def arrive(i, zd):
        mine(i, zd).wait()
        pair(i, zd).wait_recv()

    def step(i, zd, buf, sems, first, to):
        arrive(i, zd)

        @pl.when(first)
        def _():
            acc[zd, rows(i)] = both(i, zd).astype(BF16)

        @pl.when(jnp.logical_not(first))
        def _():
            pass_on(i, zd, buf, sems, to).wait_recv()
            acc[zd, rows(i)] = (both(i, zd) + buf[zd, rows(i)].astype(F32)).astype(BF16)

        pass_on(i, zd, buf, sems, to).start()

    def sums(i, k):
        rd, ld = chips - 1 - k, k
        when(rd > z, functools.partial(step, i, rd, from_l, fl_r, z == 0, me + 2))
        when(ld < z, functools.partial(step, i, ld, from_r, fr_r, z == chips - 1, me - 2))

    first = [
        Line(chips, lambda j, i=i: att.at[j, rows(i)], g1_r.at[i], g1_a.at[i], g1_b.at[i], g1_c.at[i])
        for i in range(chunks)
    ]
    second = [
        Line(chips, lambda j, i=i: hcol.at[j, i], g2_r.at[i], g2_a.at[i], g2_b.at[i], g2_c.at[i])
        for i in range(chunks)
    ]

    def attended(i):
        arrive(i, z)
        tot[...] = both(i, z)

        @pl.when(z > 0)
        def _():
            pass_on(i, z, from_l, fl_r, me).wait_recv()
            tot[...] += from_l[z, rows(i)].astype(F32)

        @pl.when(z < chips - 1)
        def _():
            pass_on(i, z, from_r, fr_r, me).wait_recv()
            tot[...] += from_r[z, rows(i)].astype(F32)

        for h in range(HEADS):
            cols = slice(h * hd, (h + 1) * hd)
            att[me, rows(i), cols] = (tot[:, cols] / tot[:, width + h : width + h + 1]).astype(BF16)
        first[i].start()

    def project(i):
        first[i].arrive()
        if i == 0:
            for k in range(1, groups):
                w_dp(k, lax.rem(grp + groups - k, groups)).wait_recv()
        projected = jnp.dot(
            att[:, rows(i), :].reshape(shards * CHUNK, width),
            wcol[...].reshape(width, ncol),
            preferred_element_type=F32,
        )
        res = res_ref[:, rows(i), :].reshape(shards * CHUNK, ncol)
        hcol[me, i] = (res.astype(F32) + projected).astype(BF16)
        second[i].start()

    def total_copy(i, n):
        return pltpu.make_async_remote_copy(
            src_ref=stats.at[i], dst_ref=slots.at[n, i], send_sem=t_s.at[i, n],
            recv_sem=t_r.at[i, n], device_id={"mp": lax.rem(me + n, shards)}, device_id_type=MESH,
        )

    def score(i):
        count = shards * CHUNK
        h = out_ref[:, rows(i), :].reshape(count, width).astype(F32)
        normed = (
            h * lax.rsqrt(jnp.mean(h * h, -1, keepdims=True) + 1e-06) * gain_ref[...]
        ).astype(BF16)
        lane = lax.broadcasted_iota(jnp.int32, (count, 128), 1)
        mark = mark_ref[:, rows(i), :].reshape(count, 128)
        marks = [mark[:, n : n + 1] for n in range(3)]
        new = [jnp.zeros((count, 128), F32) for _ in range(4)]
        vocab = vbuf.shape[1]
        for low in range(0, vocab, 512):
            high = min(low + 512, vocab)
            logits = jnp.dot(normed, vbuf[:, low:high], preferred_element_type=F32)
            for b in range(0, high - low, 128):
                x = logits[:, b : b + 128]
                new[0] += jnp.exp(x)
                for n in range(3):
                    new[n + 1] += jnp.where(lane + (low + b) == marks[n], x, 0.0)
        stat = jnp.zeros((count, 128), F32)
        for n in range(4):
            stat = jnp.where(lane == n, jnp.sum(new[n], -1, keepdims=True), stat)
        stats[i] = jnp.transpose(stat)[:8]
        for n in range(1, shards):
            total_copy(i, n).start()

    def place(i):
        second[i].arrive()
        for j in range(shards):
            for t in range(shards):
                out_ref[t, rows(i), j * ncol : (j + 1) * ncol] = hcol[
                    j, i, t * CHUNK : (t + 1) * CHUNK
                ]

    for k in range(chips - 1):
        for i in range(chunks):
            sums(i, k)
        if k == 0:
            for n in range(1, shards):
                w_mp(n).start()
    for i in range(chunks):
        attended(i)
    for n in range(1, shards):
        w_mp(n).wait_recv()
    own_w.wait()
    for n in range(1, groups):
        w_dp(n, grp).start()
    for k in range(1, chips):
        for i in range(chunks):
            first[i].forward(k)
    for i in range(chunks):
        project(i)
    for k in range(1, chips - 1):
        for i in range(chunks):
            second[i].forward(k)
    for i in range(chunks):
        second[i].forward(chips - 1)
        place(i)
        if i == 0:
            load_vocab.wait()
        score(i)
    for i in range(chunks):
        total = stats[i]
        for n in range(1, shards):
            total_copy(i, n).wait_recv()
            total = total + slots[n, i]
        stat_ref[i] = total

    for i in range(chunks):
        first[i].finish()
        second[i].finish()
        for zd in range(chips):
            pair(i, zd).wait_send()
            when(zd != z, lambda: pass_on(i, zd, from_l, fl_r, me).wait_send())
    for k in range(1, shards):
        w_mp(k).wait_send()
    for k in range(1, groups):
        w_dp(k, grp).wait_send()
    for i in range(chunks):
        for n in range(1, shards):
            total_copy(i, n).wait_send()


def hidden_of(shards, groups, part, out_weight, res, gain, marks, vocab_weight):
    own, width = part.shape[1], out_weight.shape[1]
    wide = part.shape[2]
    ncol = width // shards
    chips = shards // 2
    chunks = own // CHUNK
    dma = pltpu.SemaphoreType.DMA
    anywhere = pl.BlockSpec(memory_space=pl.ANY)
    gather_sems = [dma((chunks, shards))] + [dma((chunks, chips))] * 3
    vmem = pl.BlockSpec(memory_space=pltpu.VMEM)
    return pl.pallas_call(
        functools.partial(hidden_kernel, chips, groups),
        in_specs=[anywhere, vmem, vmem, vmem, vmem, anywhere],
        out_specs=[vmem, vmem],
        out_shape=[
            jax.ShapeDtypeStruct((shards, own, width), BF16),
            jax.ShapeDtypeStruct((chunks, 8, shards * CHUNK), F32),
        ],
        scratch_shapes=[
            pltpu.VMEM((chips, own, wide), BF16),
            pltpu.VMEM((chips, own, wide), BF16),
            pltpu.VMEM((chips, own, wide), BF16),
            pltpu.VMEM((chips, own, wide), BF16),
            pltpu.VMEM((chips, own, wide), BF16),
            pltpu.VMEM((CHUNK, wide), F32),
            pltpu.VMEM((shards, own, width), BF16),
            pltpu.VMEM((groups, shards, out_weight.shape[0], ncol), BF16),
            pltpu.VMEM((shards, chunks, shards * CHUNK, ncol), BF16),
            *[dma((chunks, chips))] * 6,
            *gather_sems,
            *gather_sems,
            dma((shards,)), dma((shards,)), dma((groups,)), dma((groups,)), dma,
            pltpu.VMEM(vocab_weight.shape, BF16),
            pltpu.VMEM((chunks, 8, shards * CHUNK), F32),
            pltpu.VMEM((shards, chunks, 8, shards * CHUNK), F32),
            dma((chunks, shards)), dma((chunks, shards)), dma,
        ],
        compiler_params=pltpu.CompilerParams(
            collective_id=0, has_side_effects=True, vmem_limit_bytes=VMEM_LIMIT
        ),
        name="hidden_exchange",
    )(part, out_weight, res, gain, marks, vocab_weight)


def local_fast(
    queries, new_keys, new_values, cache_keys, cache_values, lengths, parents, tree_tokens,
    residual, out_weight, norm_gain, vocab_weight,
):
    reqs, tree, width = queries.shape
    tokens = reqs * tree
    shard = lax.axis_index("mp")
    shards = lax.axis_size("mp")
    groups = lax.axis_size("dp")
    ncol = width // shards
    part = attention(
        shards, queries, new_keys, new_values, cache_keys, cache_values, lengths, parents
    ).reshape(shards, tokens // shards, width + 128)
    res = lax.dynamic_slice_in_dim(residual.reshape(tokens, width), shard * ncol, ncol, 1)
    res = res.reshape(shards, tokens // shards, ncol)
    vocab = vocab_weight.shape[1]
    column = tree_tokens - shard * vocab
    column = jnp.where((column >= 0) & (column < vocab), column, -1)
    idx = jnp.arange(tree, dtype=jnp.int32)[None, :]
    by_one = (parents == idx - 1) & (idx > 0)
    by_two = (parents == idx - 2) & (idx > 1)

    def ahead(x, n):
        return jnp.pad(x[:, n:], ((0, 0), (0, n)), constant_values=-1)

    first = jnp.where(idx == 0, column, -1)
    marks = jnp.stack(
        [ahead(jnp.where(by_one, column, -1), 1), ahead(jnp.where(by_two, column, -1), 2), first], -1
    ).reshape(tokens, 3)
    marks = jnp.pad(marks, ((0, 0), (0, 125)), constant_values=-1)
    own = tokens // shards
    hidden, stats = hidden_of(
        shards, groups, part, out_weight, res, norm_gain.reshape(1, width),
        marks.reshape(shards, own, 128), vocab_weight,
    )
    total = stats.reshape(own // CHUNK, 8, shards, CHUNK).transpose(1, 2, 0, 3)
    total = total.reshape(8, reqs, tree)

    def behind(x, n):
        return jnp.pad(x[:, : tree - n], ((0, 0), (n, 0)))

    sums = total[0]
    picked = jnp.where(idx == 0, total[3], jnp.where(by_one, behind(total[1], 1), behind(total[2], 2)))
    norm = jnp.where(idx == 0, sums, jnp.where(by_one, behind(sums, 1), behind(sums, 2)))
    return (hidden.reshape(reqs, tree, width), picked - jnp.log(norm))


def local_plain(
    queries,
    new_keys,
    new_values,
    cache_keys,
    cache_values,
    lengths,
    parents,
    tree_tokens,
    residual,
    out_weight,
    norm_gain,
    vocab_weight,
):
    reqs, tree, width = queries.shape
    slots = cache_keys.shape[1]
    head_dim = width // HEADS
    scale = head_dim ** (-0.5)
    shard = lax.axis_index("mp")
    shards = lax.axis_size("mp")
    tokens = reqs * tree
    window = slots * shards // 2
    positions = shard * slots + jnp.arange(slots, dtype=jnp.int32)
    visible = (positions[None, :] < lengths[:, None]) & (
        (positions[None, :] < SINK) | (positions[None, :] >= lengths[:, None] - window)
    )
    q4 = queries.reshape(reqs, tree, HEADS, head_dim)
    k4 = cache_keys.reshape(reqs, slots, HEADS, head_dim)
    v4 = cache_values.reshape(reqs, slots, HEADS, head_dim)
    cache_e = jnp.where(
        visible[:, None, None, :],
        jnp.exp(jnp.einsum("rihd,rshd->rhis", q4, k4, preferred_element_type=jnp.float32) * scale),
        0.0,
    )
    cache_den = jnp.sum(cache_e, -1)
    cache_num = jnp.einsum(
        "rhis,rshd->rihd", cache_e.astype(jnp.bfloat16), v4, preferred_element_type=jnp.float32
    )
    ancestors = ancestor_mask(parents)
    nk4 = new_keys.reshape(reqs, tree, HEADS, head_dim)
    nv4 = new_values.reshape(reqs, tree, HEADS, head_dim)
    tree_e = jnp.where(
        ancestors[:, None],
        jnp.exp(jnp.einsum("rihd,rjhd->rhij", q4, nk4, preferred_element_type=jnp.float32) * scale),
        0.0,
    )
    tree_den = jnp.sum(tree_e, -1)
    tree_num = jnp.einsum(
        "rhij,rjhd->rihd", tree_e.astype(jnp.bfloat16), nv4, preferred_element_type=jnp.float32
    )
    flat_res = residual.reshape(tokens, width)
    num_all, den_all = lax.psum((cache_num.reshape(tokens, width), cache_den), "mp")
    denom = jnp.transpose(den_all + tree_den, (0, 2, 1))
    numer = num_all.reshape(reqs, tree, HEADS, head_dim) + tree_num
    attended = (numer / denom[..., None]).astype(jnp.bfloat16).reshape(tokens, width)
    projected = jnp.dot(
        attended,
        lax.all_gather(out_weight, ("dp", "mp"), axis=0, tiled=True),
        preferred_element_type=jnp.float32,
    )
    hidden = (flat_res.astype(jnp.float32) + projected).astype(jnp.bfloat16)
    hfloat = hidden.astype(jnp.float32)
    normed = (
        hfloat * lax.rsqrt(jnp.mean(hfloat * hfloat, -1, keepdims=True) + 1e-06) * norm_gain
    ).astype(jnp.bfloat16)
    vocab_dev = vocab_weight.shape[1]
    logits = jnp.dot(normed, vocab_weight, preferred_element_type=jnp.float32)
    exp_sums = jnp.sum(jnp.exp(logits), -1)
    parent_rows = (jnp.arange(reqs, dtype=jnp.int32)[:, None] * tree + parents).reshape(-1)
    column = tree_tokens.reshape(-1) - shard * vocab_dev
    inside = (column >= 0) & (column < vocab_dev)
    picked = jnp.where(inside, logits[parent_rows, jnp.clip(column, 0, vocab_dev - 1)], 0.0)
    parent_sums = exp_sums[parent_rows]
    total_sums, total_picked = lax.psum((parent_sums, picked), "mp")
    node_logprob = (total_picked - jnp.log(total_sums)).reshape(reqs, tree)
    return (hidden.reshape(reqs, tree, width), node_logprob)


def local(*args):
    queries, vocab_weight = args[0], args[-1]
    reqs, tree, width = queries.shape
    shards = lax.axis_size("mp")
    fits = (
        (reqs * tree) % (shards * 16) == 0
        and width % (shards * 128) == 0
        and width == HEADS * 128
        and tree % 16 == 0
        and vocab_weight.shape[1] % 128 == 0
        and shards % 2 == 0
        and shards >= 8
    )
    return (local_fast if fits else local_plain)(*args)


def solution(mesh):
    placed = (
        P("dp", None, None),
        P("dp", None, None),
        P("dp", None, None),
        P("dp", "mp", None),
        P("dp", "mp", None),
        P("dp"),
        P("dp", None),
        P("dp", None),
        P("dp", None, None),
        P(("dp", "mp"), None),
        P(),
        P(None, "mp"),
    )
    return jax.shard_map(
        local,
        mesh=mesh,
        in_specs=placed,
        out_specs=(P("dp", None, None), P("dp", None)),
        check_vma=False,
    )
```

```python
import functools

import jax
import jax.numpy as jnp
from jax import lax
from jax.experimental import pallas as pl
from jax.experimental.pallas import tpu as pltpu
from jax.sharding import PartitionSpec as P

HEADS = 16
SINK = 4
F32 = jnp.float32
BF16 = jnp.bfloat16
MESH = pl.DeviceIdType.MESH
VMEM_LIMIT = 56 * 1024 * 1024


def ancestor_mask(parents):
    tree = parents.shape[-1]
    idx = jnp.arange(tree, dtype=jnp.int32)
    links = (
        (idx[None, :, None] == idx[None, None, :]) | (parents[:, :, None] == idx[None, None, :])
    ).astype(F32)
    for _ in range((tree - 1).bit_length()):
        links = jnp.minimum(
            jnp.einsum("rij,rjk->rik", links, links, precision=lax.Precision.HIGHEST), 1.0
        )
    return links > 0.5


def attend(q_ref, keys, values, mask, o_ref, req):
    tree, width = q_ref.shape[1:]
    hd = width // HEADS
    scale = hd ** (-0.5)
    lane = lax.broadcasted_iota(jnp.int32, (tree, 128), 1)
    low = lax.broadcasted_iota(jnp.int32, (tree, 2 * hd), 1) < hd
    mask2 = jnp.concatenate([mask, mask], 0)
    den = jnp.zeros((tree, 128), F32)
    pairs = HEADS // 2
    for group in range(0, pairs, 4):
        scores = []
        for p in range(group, group + 4):
            cols = slice(2 * p * hd, 2 * (p + 1) * hd)
            q = q_ref[req, :, cols]
            both = jnp.concatenate(
                [jnp.where(low, q, jnp.zeros_like(q)), jnp.where(low, jnp.zeros_like(q), q)], 0
            )
            scores.append(
                lax.dot_general(
                    both, keys[req, :, cols], (((1,), (1,)), ((), ())),
                    preferred_element_type=F32,
                )
            )
        es = [jnp.where(mask2 > 0.5, jnp.exp(s * scale), 0.0) for s in scores]
        for n, e in enumerate(es):
            p = group + n
            cols = slice(2 * p * hd, 2 * (p + 1) * hd)
            num = jnp.dot(e.astype(BF16), values[req, :, cols], preferred_element_type=F32)
            o_ref[req, :, 2 * p * hd : (2 * p + 1) * hd] = num[:tree, :hd].astype(BF16)
            o_ref[req, :, (2 * p + 1) * hd : 2 * (p + 1) * hd] = num[tree:, hd:].astype(BF16)
            d = jnp.sum(e, -1, keepdims=True)
            den = jnp.where(lane == 2 * p, d[:tree], den)
            den = jnp.where(lane == 2 * p + 1, d[tree:], den)
    o_ref[req, :, width:] = den.astype(BF16)


def ancestors(par, chain):
    node = lax.broadcasted_iota(jnp.int32, (par.shape[0], 128), 1)
    rows = []
    for j in range(par.shape[1]):
        row = jnp.where(node == j, 1.0, 0.0)
        if j == 1:
            row = row + rows[0]
        elif j > 1:
            row = row + jnp.where(par[:, j : j + 1] == j - 1, rows[j - 1], rows[j - 2])
        rows.append(row)
        chain[j] = row


def when(cond, fn):
    pl.when(cond)(fn)


class Line:
    def __init__(self, chips, at, recv, send_r, send_l, send_s):
        me = lax.axis_index("mp")
        self.chips, self.at, self.recv = chips, at, recv
        self.sends = send_r, send_l, send_s
        self.me, self.c, self.z = me, lax.rem(me, 2), lax.div(me, 2)
        self.sib = 2 * self.z + 1 - self.c

    def copy(self, slot, sem, to):
        return pltpu.make_async_remote_copy(
            src_ref=self.at(slot), dst_ref=self.at(slot), send_sem=sem,
            recv_sem=self.recv.at[slot], device_id={"mp": to}, device_id_type=MESH,
        )

    def right(self, k):
        return self.copy(2 * (self.z - k) + self.c, self.sends[0].at[k], self.me + 2)

    def left(self, k):
        return self.copy(2 * (self.z + k) + self.c, self.sends[1].at[k], self.me - 2)

    def pair(self, zs):
        return self.copy(2 * zs + self.c, self.sends[2].at[zs], self.sib)

    def start(self):
        when(self.z < self.chips - 1, lambda: self.right(0).start())
        when(self.z > 0, lambda: self.left(0).start())
        self.pair(self.z).start()

    def forward(self, k):
        z, chips = self.z, self.chips

        @pl.when(z - k >= 0)
        def _():
            self.right(k).wait_recv()
            when(z < chips - 1, lambda: self.right(k).start())
            self.pair(z - k).start()

        @pl.when(z + k <= chips - 1)
        def _():
            self.left(k).wait_recv()
            when(z > 0, lambda: self.left(k).start())
            self.pair(z + k).start()

    def arrive(self):
        for zs in range(self.chips):
            self.copy(2 * zs + 1 - self.c, self.sends[2].at[zs], self.sib).wait_recv()

    def finish(self):
        z, chips = self.z, self.chips
        for k in range(chips):
            when((z - k >= 0) & (z < chips - 1), lambda: self.right(k).wait_send())
            when((z + k <= chips - 1) & (z > 0), lambda: self.left(k).wait_send())
        for zs in range(chips):
            self.pair(zs).wait_send()


CHUNK = 16


def hidden_kernel(
    chips, groups, len_ref, q_hbm, k_hbm, v_hbm, nk_hbm, nv_hbm, par_hbm, tok_hbm, res_hbm,
    w_ref, gain_ref, vocab_ref, out_ref, stat_ref,
    q_ref, k_ref, v_ref, nk_ref, nv_ref, par_ref, tok_ref, res_ref, chain, mark, part,
    q_s, k_s, v_s0, par_s, tok_s, res_s,
    sib_buf, from_l, from_r, acc, tot, att, wcol, hcol,
    sib_s, sib_r, fl_r, fr_r, acc_s, g1_r, g1_a, g1_b, g1_c, g2_r, g2_a, g2_b, g2_c,
    w1_s, w1_r, w2_s, w2_r, wown_s, vbuf, stats, slots, t_s, t_r, v_s,
):
    shards = 2 * chips
    me = lax.axis_index("mp")
    grp = lax.axis_index("dp")
    c, z = lax.rem(me, 2), lax.div(me, 2)
    sib = 2 * z + 1 - c
    width = att.shape[-1]
    tree = q_ref.shape[1]
    span = k_ref.shape[1]
    cap = span * shards
    hd = width // HEADS
    ncol = wcol.shape[-1]
    vocab = vbuf.shape[1]
    chunks = att.shape[1] // CHUNK
    tree_shard = max(shards // 8, 1)
    on_tree = me == tree_shard
    on_cache = (me < tree_shard) | (me >= shards // 2)

    def rows(i):
        return pl.ds(i * CHUNK, CHUNK)

    def columns(j):
        return pl.ds(pl.multiple_of(j * ncol, 128), ncol)

    def loads(r, keys, key_buf, values, value_buf):
        return [
            pltpu.make_async_copy(q_hbm.at[r], q_ref.at[r], q_s.at[r]),
            pltpu.make_async_copy(keys.at[r], key_buf.at[r], k_s.at[r]),
            pltpu.make_async_copy(values.at[r], value_buf.at[r], v_s0.at[r]),
        ]

    def cache_loads(r):
        return loads(r, k_hbm, k_ref, v_hbm, v_ref)

    def tree_loads(r):
        return loads(r, nk_hbm, nk_ref, nv_hbm, nv_ref)

    barrier = pltpu.get_barrier_semaphore()
    for k in range(1, shards):
        pl.semaphore_signal(
            barrier, inc=1, device_id={"mp": lax.rem(me + k, shards)}, device_id_type=MESH
        )
    for k in range(1, groups):
        pl.semaphore_signal(
            barrier, inc=1, device_id={"dp": lax.rem(grp + k, groups)}, device_id_type=MESH
        )

    order = []
    for k in range(chips):
        for zd in (chips - 1 - k, k):
            if zd not in order:
                order.append(zd)

    load_par = pltpu.make_async_copy(par_hbm, par_ref, par_s)
    load_tok = pltpu.make_async_copy(tok_hbm, tok_ref, tok_s)
    load_par.start()
    load_tok.start()
    for zd in order:
        for r in (2 * zd, 2 * zd + 1):
            when(on_cache, lambda: [x.start() for x in cache_loads(r)] and None)
            when(on_tree, lambda: [x.start() for x in tree_loads(r)] and None)
    own_w = pltpu.make_async_copy(w_ref.at[:, columns(me)], wcol.at[grp, me], wown_s)
    own_w.start()
    load_res = pltpu.make_async_copy(res_hbm.at[:, :, columns(me)], res_ref, res_s)
    load_res.start()
    load_vocab = pltpu.make_async_copy(vocab_ref, vbuf, v_s)
    load_vocab.start()

    load_par.wait()
    load_tok.wait()
    when(on_tree, lambda: ancestors(par_ref[...], chain))

    idx = lax.broadcasted_iota(jnp.int32, par_ref.shape, 1)
    column = tok_ref[...] - me * vocab
    column = jnp.where((column >= 0) & (column < vocab), column, -1)
    mark[...] = jnp.full(mark.shape, -1.0, F32)
    mark[0:8, 0:tree] = jnp.where((par_ref[...] == idx - 1) & (idx > 0), column, -1).astype(F32)
    mark[8:16, 0:tree] = jnp.where((par_ref[...] == idx - 2) & (idx > 1), column, -1).astype(F32)
    mark[16:24, 0:tree] = jnp.where(idx == 0, column, -1).astype(F32)
    mark[...] = jnp.transpose(mark[...])

    pl.semaphore_wait(barrier, shards - 1 + groups - 1)

    def pair(i, zd):
        return pltpu.make_async_remote_copy(
            src_ref=part.at[2 * zd + 1 - c, rows(i)], dst_ref=sib_buf.at[zd, rows(i)],
            send_sem=sib_s.at[i, zd], recv_sem=sib_r.at[i, zd],
            device_id={"mp": sib}, device_id_type=MESH,
        )

    def w_mp(k):
        to = lax.rem(me + k, shards)
        return pltpu.make_async_remote_copy(
            src_ref=w_ref.at[:, columns(to)], dst_ref=wcol.at[grp, me], send_sem=w1_s.at[k],
            recv_sem=w1_r.at[k], device_id={"mp": to}, device_id_type=MESH,
        )

    def w_dp(k, src):
        return pltpu.make_async_remote_copy(
            src_ref=wcol.at[src], dst_ref=wcol.at[src], send_sem=w2_s.at[k],
            recv_sem=w2_r.at[k], device_id={"dp": lax.rem(grp + k, groups)}, device_id_type=MESH,
        )

    for n in range(1, shards):
        w_mp(n).start()

    def one_request(n, carry):
        k = lax.div(n, 2)
        zd = jnp.where(lax.rem(k, 2) == 0, chips - 1 - lax.div(k, 2), lax.div(k, 2))
        r = 2 * zd + lax.rem(n, 2)

        @pl.when(on_cache)
        def _():
            for x in cache_loads(r):
                x.wait()
            length = len_ref[r]
            pos = me * span + lax.broadcasted_iota(jnp.int32, (tree, span), 1)
            mask = (pos < length) & ((pos < SINK) | (pos >= length - cap // 2))
            attend(q_ref, k_ref, v_ref, jnp.where(mask, 1.0, 0.0), part, r)

        @pl.when(on_tree)
        def _():
            for x in tree_loads(r):
                x.wait()
            attend(q_ref, nk_ref, nv_ref, chain[:, r, :][:, :tree], part, r)

        @pl.when(jnp.logical_not(on_cache | on_tree))
        def _():
            part[r] = jnp.zeros(part.shape[1:], BF16)

        @pl.when(lax.rem(n, 2) != c)
        def _():
            for i in range(chunks):
                pair(i, zd).start()

        return carry

    lax.fori_loop(0, shards, one_request, 0)

    for n in range(1, shards):
        w_mp(n).wait_recv()
    own_w.wait()
    for n in range(1, groups):
        w_dp(n, grp).start()

    def pass_on(i, zd, buf, sems, to):
        return pltpu.make_async_remote_copy(
            src_ref=acc.at[zd, rows(i)], dst_ref=buf.at[zd, rows(i)], send_sem=acc_s.at[i, zd],
            recv_sem=sems.at[i, zd], device_id={"mp": to}, device_id_type=MESH,
        )

    def both(i, zd):
        return part[2 * zd + c, rows(i)].astype(F32) + sib_buf[zd, rows(i)].astype(F32)

    def arrive(i, zd):
        pair(i, zd).wait_recv()

    def step(i, zd, buf, sems, first, to):
        arrive(i, zd)

        @pl.when(first)
        def _():
            acc[zd, rows(i)] = both(i, zd).astype(BF16)

        @pl.when(jnp.logical_not(first))
        def _():
            pass_on(i, zd, buf, sems, to).wait_recv()
            acc[zd, rows(i)] = (both(i, zd) + buf[zd, rows(i)].astype(F32)).astype(BF16)

        pass_on(i, zd, buf, sems, to).start()

    def sums(i, k):
        rd, ld = chips - 1 - k, k
        when(rd > z, functools.partial(step, i, rd, from_l, fl_r, z == 0, me + 2))
        when(ld < z, functools.partial(step, i, ld, from_r, fr_r, z == chips - 1, me - 2))

    first = [
        Line(chips, lambda j, i=i: att.at[j, rows(i)], g1_r.at[i], g1_a.at[i], g1_b.at[i], g1_c.at[i])
        for i in range(chunks)
    ]
    second = [
        Line(chips, lambda j, i=i: hcol.at[j, i], g2_r.at[i], g2_a.at[i], g2_b.at[i], g2_c.at[i])
        for i in range(chunks)
    ]

    def attended(i):
        arrive(i, z)
        tot[...] = both(i, z)

        @pl.when(z > 0)
        def _():
            pass_on(i, z, from_l, fl_r, me).wait_recv()
            tot[...] += from_l[z, rows(i)].astype(F32)

        @pl.when(z < chips - 1)
        def _():
            pass_on(i, z, from_r, fr_r, me).wait_recv()
            tot[...] += from_r[z, rows(i)].astype(F32)

        for h in range(HEADS):
            cols = slice(h * hd, (h + 1) * hd)
            att[me, rows(i), cols] = (tot[:, cols] / tot[:, width + h : width + h + 1]).astype(BF16)
        first[i].start()

    def project(i):
        first[i].arrive()
        if i == 0:
            load_res.wait()
            for k in range(1, groups):
                w_dp(k, lax.rem(grp + groups - k, groups)).wait_recv()
        projected = jnp.dot(
            att[:, rows(i), :].reshape(shards * CHUNK, width),
            wcol[...].reshape(width, ncol),
            preferred_element_type=F32,
        )
        res = res_ref[:, rows(i), :].reshape(shards * CHUNK, ncol)
        hcol[me, i] = (res.astype(F32) + projected).astype(BF16)
        second[i].start()

    def total_copy(i, n):
        return pltpu.make_async_remote_copy(
            src_ref=stats.at[i], dst_ref=slots.at[n, i], send_sem=t_s.at[i, n],
            recv_sem=t_r.at[i, n], device_id={"mp": lax.rem(me + n, shards)}, device_id_type=MESH,
        )

    def score(i):
        count = shards * CHUNK
        h = out_ref[:, rows(i), :].reshape(count, width).astype(F32)
        normed = (
            h * lax.rsqrt(jnp.mean(h * h, -1, keepdims=True) + 1e-06) * gain_ref[...]
        ).astype(BF16)
        lane = lax.broadcasted_iota(jnp.int32, (count, 128), 1)
        marks = []
        for n, ahead in enumerate((1, 2, 0)):
            low = i * CHUNK + ahead
            marks.append(
                jnp.concatenate(
                    [mark[low : low + CHUNK, 8 * n + t : 8 * n + t + 1] for t in range(shards)], 0
                ).astype(jnp.int32)
            )
        new = [jnp.zeros((count, 128), F32) for _ in range(4)]
        for low in range(0, vocab, 512):
            high = min(low + 512, vocab)
            logits = jnp.dot(normed, vbuf[:, low:high], preferred_element_type=F32)
            for b in range(0, high - low, 128):
                x = logits[:, b : b + 128]
                new[0] += jnp.exp(x)
                for n in range(3):
                    new[n + 1] += jnp.where(lane + (low + b) == marks[n], x, 0.0)
        stat = jnp.zeros((count, 128), F32)
        for n in range(4):
            stat = jnp.where(lane == n, jnp.sum(new[n], -1, keepdims=True), stat)
        stats[i] = jnp.transpose(stat)[:8]
        for n in range(1, shards):
            total_copy(i, n).start()

    def place(i):
        second[i].arrive()
        for j in range(shards):
            for t in range(shards):
                out_ref[t, rows(i), j * ncol : (j + 1) * ncol] = hcol[
                    j, i, t * CHUNK : (t + 1) * CHUNK
                ]

    for k in range(chips - 1):
        for i in range(chunks):
            sums(i, k)
    for i in range(chunks):
        attended(i)
    for k in range(1, chips):
        for i in range(chunks):
            first[i].forward(k)
    for i in range(chunks):
        project(i)
    for k in range(1, chips - 1):
        for i in range(chunks):
            second[i].forward(k)
    for i in range(chunks):
        second[i].forward(chips - 1)
        place(i)
        if i == 0:
            load_vocab.wait()
        score(i)
    for i in range(chunks):
        total = stats[i]
        for n in range(1, shards):
            total_copy(i, n).wait_recv()
            total = total + slots[n, i]
        stat_ref[i] = total

    for i in range(chunks):
        first[i].finish()
        second[i].finish()
        for zd in range(chips):
            pair(i, zd).wait_send()
            when(zd != z, lambda: pass_on(i, zd, from_l, fl_r, me).wait_send())
    for k in range(1, shards):
        w_mp(k).wait_send()
    for k in range(1, groups):
        w_dp(k, grp).wait_send()
    for i in range(chunks):
        for n in range(1, shards):
            total_copy(i, n).wait_send()


def hidden_of(
    shards, groups, lengths, queries, cache_keys, cache_values, new_keys, new_values, parents,
    tree_tokens, residual, out_weight, gain, vocab_weight,
):
    own, width = queries.shape[1:]
    wide = width + 128
    ncol = width // shards
    chips = shards // 2
    chunks = own // CHUNK
    dma = pltpu.SemaphoreType.DMA
    anywhere = pl.BlockSpec(memory_space=pl.ANY)
    gather_sems = [dma((chunks, shards))] + [dma((chunks, chips))] * 3
    vmem = pl.BlockSpec(memory_space=pltpu.VMEM)
    return pl.pallas_call(
        functools.partial(hidden_kernel, chips, groups),
        in_specs=[pl.BlockSpec(memory_space=pltpu.SMEM)] + [anywhere] * 8 + [vmem, vmem, anywhere],
        out_specs=[vmem, vmem],
        out_shape=[
            jax.ShapeDtypeStruct((shards, own, width), BF16),
            jax.ShapeDtypeStruct((chunks, 8, shards * CHUNK), F32),
        ],
        scratch_shapes=[
            pltpu.VMEM(queries.shape, BF16),
            pltpu.VMEM(cache_keys.shape, BF16),
            pltpu.VMEM(cache_values.shape, BF16),
            pltpu.VMEM(new_keys.shape, BF16),
            pltpu.VMEM(new_values.shape, BF16),
            pltpu.VMEM(parents.shape, jnp.int32),
            pltpu.VMEM(tree_tokens.shape, jnp.int32),
            pltpu.VMEM((shards, own, ncol), BF16),
            pltpu.VMEM((own, shards, 128), F32),
            pltpu.VMEM((128, 128), F32),
            pltpu.VMEM((shards, own, wide), BF16),
            dma((shards,)), dma((shards,)), dma((shards,)), dma, dma, dma,
            pltpu.VMEM((chips, own, wide), BF16),
            pltpu.VMEM((chips, own, wide), BF16),
            pltpu.VMEM((chips, own, wide), BF16),
            pltpu.VMEM((chips, own, wide), BF16),
            pltpu.VMEM((CHUNK, wide), F32),
            pltpu.VMEM((shards, own, width), BF16),
            pltpu.VMEM((groups, shards, out_weight.shape[0], ncol), BF16),
            pltpu.VMEM((shards, chunks, shards * CHUNK, ncol), BF16),
            *[dma((chunks, chips))] * 5,
            *gather_sems,
            *gather_sems,
            dma((shards,)), dma((shards,)), dma((groups,)), dma((groups,)), dma,
            pltpu.VMEM(vocab_weight.shape, BF16),
            pltpu.VMEM((chunks, 8, shards * CHUNK), F32),
            pltpu.VMEM((shards, chunks, 8, shards * CHUNK), F32),
            dma((chunks, shards)), dma((chunks, shards)), dma,
        ],
        compiler_params=pltpu.CompilerParams(
            collective_id=0, has_side_effects=True, vmem_limit_bytes=VMEM_LIMIT
        ),
        name="hidden_exchange",
    )(
        lengths, queries, cache_keys, cache_values, new_keys, new_values, parents, tree_tokens,
        residual, out_weight, gain, vocab_weight,
    )


def local_fast(
    queries, new_keys, new_values, cache_keys, cache_values, lengths, parents, tree_tokens,
    residual, out_weight, norm_gain, vocab_weight,
):
    reqs, tree, width = queries.shape
    tokens = reqs * tree
    shards = lax.axis_size("mp")
    groups = lax.axis_size("dp")
    idx = jnp.arange(tree, dtype=jnp.int32)[None, :]
    by_one = (parents == idx - 1) & (idx > 0)
    own = tokens // shards
    hidden, stats = hidden_of(
        shards, groups, lengths, queries, cache_keys, cache_values, new_keys, new_values, parents,
        tree_tokens, residual, out_weight, norm_gain.reshape(1, width), vocab_weight,
    )
    total = stats.reshape(own // CHUNK, 8, shards, CHUNK).transpose(1, 2, 0, 3)
    total = total.reshape(8, reqs, tree)

    def behind(x, n):
        return jnp.pad(x[:, : tree - n], ((0, 0), (n, 0)))

    sums = total[0]
    picked = jnp.where(idx == 0, total[3], jnp.where(by_one, behind(total[1], 1), behind(total[2], 2)))
    norm = jnp.where(idx == 0, sums, jnp.where(by_one, behind(sums, 1), behind(sums, 2)))
    return (hidden.reshape(reqs, tree, width), picked - jnp.log(norm))


def local_plain(
    queries,
    new_keys,
    new_values,
    cache_keys,
    cache_values,
    lengths,
    parents,
    tree_tokens,
    residual,
    out_weight,
    norm_gain,
    vocab_weight,
):
    reqs, tree, width = queries.shape
    slots = cache_keys.shape[1]
    head_dim = width // HEADS
    scale = head_dim ** (-0.5)
    shard = lax.axis_index("mp")
    shards = lax.axis_size("mp")
    tokens = reqs * tree
    window = slots * shards // 2
    positions = shard * slots + jnp.arange(slots, dtype=jnp.int32)
    visible = (positions[None, :] < lengths[:, None]) & (
        (positions[None, :] < SINK) | (positions[None, :] >= lengths[:, None] - window)
    )
    q4 = queries.reshape(reqs, tree, HEADS, head_dim)
    k4 = cache_keys.reshape(reqs, slots, HEADS, head_dim)
    v4 = cache_values.reshape(reqs, slots, HEADS, head_dim)
    cache_e = jnp.where(
        visible[:, None, None, :],
        jnp.exp(jnp.einsum("rihd,rshd->rhis", q4, k4, preferred_element_type=jnp.float32) * scale),
        0.0,
    )
    cache_den = jnp.sum(cache_e, -1)
    cache_num = jnp.einsum(
        "rhis,rshd->rihd", cache_e.astype(jnp.bfloat16), v4, preferred_element_type=jnp.float32
    )
    ancestors = ancestor_mask(parents)
    nk4 = new_keys.reshape(reqs, tree, HEADS, head_dim)
    nv4 = new_values.reshape(reqs, tree, HEADS, head_dim)
    tree_e = jnp.where(
        ancestors[:, None],
        jnp.exp(jnp.einsum("rihd,rjhd->rhij", q4, nk4, preferred_element_type=jnp.float32) * scale),
        0.0,
    )
    tree_den = jnp.sum(tree_e, -1)
    tree_num = jnp.einsum(
        "rhij,rjhd->rihd", tree_e.astype(jnp.bfloat16), nv4, preferred_element_type=jnp.float32
    )
    flat_res = residual.reshape(tokens, width)
    num_all, den_all = lax.psum((cache_num.reshape(tokens, width), cache_den), "mp")
    denom = jnp.transpose(den_all + tree_den, (0, 2, 1))
    numer = num_all.reshape(reqs, tree, HEADS, head_dim) + tree_num
    attended = (numer / denom[..., None]).astype(jnp.bfloat16).reshape(tokens, width)
    projected = jnp.dot(
        attended,
        lax.all_gather(out_weight, ("dp", "mp"), axis=0, tiled=True),
        preferred_element_type=jnp.float32,
    )
    hidden = (flat_res.astype(jnp.float32) + projected).astype(jnp.bfloat16)
    hfloat = hidden.astype(jnp.float32)
    normed = (
        hfloat * lax.rsqrt(jnp.mean(hfloat * hfloat, -1, keepdims=True) + 1e-06) * norm_gain
    ).astype(jnp.bfloat16)
    vocab_dev = vocab_weight.shape[1]
    logits = jnp.dot(normed, vocab_weight, preferred_element_type=jnp.float32)
    exp_sums = jnp.sum(jnp.exp(logits), -1)
    parent_rows = (jnp.arange(reqs, dtype=jnp.int32)[:, None] * tree + parents).reshape(-1)
    column = tree_tokens.reshape(-1) - shard * vocab_dev
    inside = (column >= 0) & (column < vocab_dev)
    picked = jnp.where(inside, logits[parent_rows, jnp.clip(column, 0, vocab_dev - 1)], 0.0)
    parent_sums = exp_sums[parent_rows]
    total_sums, total_picked = lax.psum((parent_sums, picked), "mp")
    node_logprob = (total_picked - jnp.log(total_sums)).reshape(reqs, tree)
    return (hidden.reshape(reqs, tree, width), node_logprob)


def local(*args):
    queries, vocab_weight = args[0], args[-1]
    reqs, tree, width = queries.shape
    shards = lax.axis_size("mp")
    fits = (
        (reqs * tree) % (shards * 16) == 0
        and width % (shards * 128) == 0
        and width == HEADS * 128
        and tree % 16 == 0
        and vocab_weight.shape[1] % 128 == 0
        and shards % 2 == 0
        and shards == 8
        and reqs == shards
    )
    return (local_fast if fits else local_plain)(*args)


def solution(mesh):
    placed = (
        P("dp", None, None),
        P("dp", None, None),
        P("dp", None, None),
        P("dp", "mp", None),
        P("dp", "mp", None),
        P("dp"),
        P("dp", None),
        P("dp", None),
        P("dp", None, None),
        P(("dp", "mp"), None),
        P(),
        P(None, "mp"),
    )
    return jax.shard_map(
        local,
        mesh=mesh,
        in_specs=placed,
        out_specs=(P("dp", None, None), P("dp", None)),
        check_vma=False,
    )
```

```python
import functools

import jax
import jax.numpy as jnp
from jax import lax
from jax.experimental import pallas as pl
from jax.experimental.pallas import tpu as pltpu
from jax.sharding import PartitionSpec as P

HEADS = 16
SINK = 4
F32 = jnp.float32
BF16 = jnp.bfloat16
MESH = pl.DeviceIdType.MESH
VMEM_LIMIT = 56 * 1024 * 1024


def ancestor_mask(parents):
    tree = parents.shape[-1]
    idx = jnp.arange(tree, dtype=jnp.int32)
    links = (
        (idx[None, :, None] == idx[None, None, :]) | (parents[:, :, None] == idx[None, None, :])
    ).astype(F32)
    for _ in range((tree - 1).bit_length()):
        links = jnp.minimum(
            jnp.einsum("rij,rjk->rik", links, links, precision=lax.Precision.HIGHEST), 1.0
        )
    return links > 0.5


def attend(q_ref, keys, values, mask, o_ref, req):
    tree, width = q_ref.shape[1:]
    hd = width // HEADS
    scale = hd ** (-0.5)
    lane = lax.broadcasted_iota(jnp.int32, (tree, 128), 1)
    low = lax.broadcasted_iota(jnp.int32, (tree, 2 * hd), 1) < hd
    mask2 = jnp.concatenate([mask, mask], 0)
    den = jnp.zeros((tree, 128), F32)
    pairs = HEADS // 2
    for group in range(0, pairs, 4):
        scores = []
        for p in range(group, group + 4):
            cols = slice(2 * p * hd, 2 * (p + 1) * hd)
            q = q_ref[req, :, cols]
            both = jnp.concatenate(
                [jnp.where(low, q, jnp.zeros_like(q)), jnp.where(low, jnp.zeros_like(q), q)], 0
            )
            scores.append(
                lax.dot_general(
                    both, keys[req, :, cols], (((1,), (1,)), ((), ())),
                    preferred_element_type=F32,
                )
            )
        es = [jnp.where(mask2 > 0.5, jnp.exp(s * scale), 0.0) for s in scores]
        for n, e in enumerate(es):
            p = group + n
            cols = slice(2 * p * hd, 2 * (p + 1) * hd)
            num = jnp.dot(e.astype(BF16), values[req, :, cols], preferred_element_type=F32)
            o_ref[req, :, 2 * p * hd : (2 * p + 1) * hd] = num[:tree, :hd].astype(BF16)
            o_ref[req, :, (2 * p + 1) * hd : 2 * (p + 1) * hd] = num[tree:, hd:].astype(BF16)
            d = jnp.sum(e, -1, keepdims=True)
            den = jnp.where(lane == 2 * p, d[:tree], den)
            den = jnp.where(lane == 2 * p + 1, d[tree:], den)
    o_ref[req, :, width:] = den.astype(BF16)


def ancestors(par, chain):
    node = lax.broadcasted_iota(jnp.int32, (par.shape[0], 128), 1)
    rows = []
    for j in range(par.shape[1]):
        row = jnp.where(node == j, 1.0, 0.0)
        if j == 1:
            row = row + rows[0]
        elif j > 1:
            row = row + jnp.where(par[:, j : j + 1] == j - 1, rows[j - 1], rows[j - 2])
        rows.append(row)
        chain[j] = row


def when(cond, fn):
    pl.when(cond)(fn)


class Line:
    def __init__(self, chips, at, recv, send_r, send_l, send_s):
        me = lax.axis_index("mp")
        self.chips, self.at, self.recv = chips, at, recv
        self.sends = send_r, send_l, send_s
        self.me, self.c, self.z = me, lax.rem(me, 2), lax.div(me, 2)
        self.sib = 2 * self.z + 1 - self.c

    def copy(self, slot, sem, to):
        return pltpu.make_async_remote_copy(
            src_ref=self.at(slot), dst_ref=self.at(slot), send_sem=sem,
            recv_sem=self.recv.at[slot], device_id={"mp": to}, device_id_type=MESH,
        )

    def right(self, k):
        return self.copy(2 * (self.z - k) + self.c, self.sends[0].at[k], self.me + 2)

    def left(self, k):
        return self.copy(2 * (self.z + k) + self.c, self.sends[1].at[k], self.me - 2)

    def pair(self, zs):
        return self.copy(2 * zs + self.c, self.sends[2].at[zs], self.sib)

    def start(self):
        when(self.z < self.chips - 1, lambda: self.right(0).start())
        when(self.z > 0, lambda: self.left(0).start())
        self.pair(self.z).start()

    def forward(self, k):
        z, chips = self.z, self.chips

        @pl.when(z - k >= 0)
        def _():
            self.right(k).wait_recv()
            when(z < chips - 1, lambda: self.right(k).start())
            self.pair(z - k).start()

        @pl.when(z + k <= chips - 1)
        def _():
            self.left(k).wait_recv()
            when(z > 0, lambda: self.left(k).start())
            self.pair(z + k).start()

    def arrive(self):
        for zs in range(self.chips):
            self.copy(2 * zs + 1 - self.c, self.sends[2].at[zs], self.sib).wait_recv()

    def finish(self):
        z, chips = self.z, self.chips
        for k in range(chips):
            when((z - k >= 0) & (z < chips - 1), lambda: self.right(k).wait_send())
            when((z + k <= chips - 1) & (z > 0), lambda: self.left(k).wait_send())
        for zs in range(chips):
            self.pair(zs).wait_send()


CHUNK = 16


def hidden_kernel(
    chips, groups, len_ref, q_hbm, k_hbm, v_hbm, nk_hbm, nv_hbm, par_hbm, tok_hbm, res_hbm,
    w_ref, gain_ref, vocab_ref, out_ref, stat_ref,
    q_ref, k_ref, v_ref, nk_ref, nv_ref, par_ref, tok_ref, res_ref, chain, mark, part,
    q_s, k_s, v_s0, par_s, tok_s, res_s,
    sib_buf, from_l, from_r, acc, tot, att, wcol, hcol,
    sib_s, sib_r, fl_r, fr_r, acc_s, g1_r, g1_a, g1_b, g1_c, g2_r, g2_a, g2_b, g2_c,
    w1_s, w1_r, w2_s, w2_r, wown_s, vbuf, stats, slots, t_s, t_r, v_s,
):
    shards = 2 * chips
    me = lax.axis_index("mp")
    grp = lax.axis_index("dp")
    c, z = lax.rem(me, 2), lax.div(me, 2)
    sib = 2 * z + 1 - c
    width = att.shape[-1]
    tree = q_ref.shape[1]
    span = k_ref.shape[1]
    cap = span * shards
    hd = width // HEADS
    ncol = wcol.shape[-1]
    vocab = vbuf.shape[1]
    chunks = att.shape[1] // CHUNK
    tree_shard = max(shards // 8, 1)
    on_tree = me == tree_shard
    on_cache = (me < tree_shard) | (me >= shards // 2)

    def rows(i):
        return pl.ds(i * CHUNK, CHUNK)

    def columns(j):
        return pl.ds(pl.multiple_of(j * ncol, 128), ncol)

    def loads(r, keys, key_buf, values, value_buf):
        return [
            pltpu.make_async_copy(q_hbm.at[r], q_ref.at[r], q_s.at[r]),
            pltpu.make_async_copy(keys.at[r], key_buf.at[r], k_s.at[r]),
            pltpu.make_async_copy(values.at[r], value_buf.at[r], v_s0.at[r]),
        ]

    def cache_loads(r):
        return loads(r, k_hbm, k_ref, v_hbm, v_ref)

    def tree_loads(r):
        return loads(r, nk_hbm, nk_ref, nv_hbm, nv_ref)

    barrier = pltpu.get_barrier_semaphore()
    for k in range(1, shards):
        pl.semaphore_signal(
            barrier, inc=1, device_id={"mp": lax.rem(me + k, shards)}, device_id_type=MESH
        )
    for k in range(1, groups):
        pl.semaphore_signal(
            barrier, inc=1, device_id={"dp": lax.rem(grp + k, groups)}, device_id_type=MESH
        )

    order = []
    for k in range(chips):
        for zd in (chips - 1 - k, k):
            if zd not in order:
                order.append(zd)

    load_par = pltpu.make_async_copy(par_hbm, par_ref, par_s)
    load_tok = pltpu.make_async_copy(tok_hbm, tok_ref, tok_s)
    load_par.start()
    load_tok.start()
    for zd in order:
        for r in (2 * zd, 2 * zd + 1):
            when(on_cache, lambda: [x.start() for x in cache_loads(r)] and None)
            when(on_tree, lambda: [x.start() for x in tree_loads(r)] and None)
    own_w = pltpu.make_async_copy(w_ref.at[:, columns(me)], wcol.at[grp, me], wown_s)
    own_w.start()
    load_res = pltpu.make_async_copy(res_hbm.at[:, :, columns(me)], res_ref, res_s)
    load_res.start()
    load_vocab = pltpu.make_async_copy(vocab_ref, vbuf, v_s)
    load_vocab.start()

    load_par.wait()
    load_tok.wait()
    when(on_tree, lambda: ancestors(par_ref[...], chain))

    idx = lax.broadcasted_iota(jnp.int32, par_ref.shape, 1)
    column = tok_ref[...] - me * vocab
    column = jnp.where((column >= 0) & (column < vocab), column, -1)
    mark[...] = jnp.full(mark.shape, -1.0, F32)
    mark[0:8, 0:tree] = jnp.where((par_ref[...] == idx - 1) & (idx > 0), column, -1).astype(F32)
    mark[8:16, 0:tree] = jnp.where((par_ref[...] == idx - 2) & (idx > 1), column, -1).astype(F32)
    mark[16:24, 0:tree] = jnp.where(idx == 0, column, -1).astype(F32)
    mark[...] = jnp.transpose(mark[...])

    pl.semaphore_wait(barrier, shards - 1 + groups - 1)

    def pair(i, zd):
        return pltpu.make_async_remote_copy(
            src_ref=part.at[2 * zd + 1 - c, rows(i)], dst_ref=sib_buf.at[zd, rows(i)],
            send_sem=sib_s.at[i, zd], recv_sem=sib_r.at[i, zd],
            device_id={"mp": sib}, device_id_type=MESH,
        )

    def w_mp(k):
        to = lax.rem(me + k, shards)
        return pltpu.make_async_remote_copy(
            src_ref=w_ref.at[:, columns(to)], dst_ref=wcol.at[grp, me], send_sem=w1_s.at[k],
            recv_sem=w1_r.at[k], device_id={"mp": to}, device_id_type=MESH,
        )

    def w_dp(k, src):
        return pltpu.make_async_remote_copy(
            src_ref=wcol.at[src], dst_ref=wcol.at[src], send_sem=w2_s.at[k],
            recv_sem=w2_r.at[k], device_id={"dp": lax.rem(grp + k, groups)}, device_id_type=MESH,
        )

    for n in range(1, shards):
        w_mp(n).start()

    def one_request(n, carry):
        k = lax.div(n, 2)
        zd = jnp.where(lax.rem(k, 2) == 0, chips - 1 - lax.div(k, 2), lax.div(k, 2))
        r = 2 * zd + lax.rem(n, 2)

        @pl.when(on_cache)
        def _():
            for x in cache_loads(r):
                x.wait()
            length = len_ref[r]
            pos = me * span + lax.broadcasted_iota(jnp.int32, (tree, span), 1)
            mask = (pos < length) & ((pos < SINK) | (pos >= length - cap // 2))
            attend(q_ref, k_ref, v_ref, jnp.where(mask, 1.0, 0.0), part, r)

        @pl.when(on_tree)
        def _():
            for x in tree_loads(r):
                x.wait()
            attend(q_ref, nk_ref, nv_ref, chain[:, r, :][:, :tree], part, r)

        @pl.when(jnp.logical_not(on_cache | on_tree))
        def _():
            part[r] = jnp.zeros(part.shape[1:], BF16)

        @pl.when(lax.rem(n, 2) != c)
        def _():
            for i in range(chunks):
                pair(i, zd).start()

        return carry

    lax.fori_loop(0, shards, one_request, 0)

    for n in range(1, shards):
        w_mp(n).wait_recv()
    own_w.wait()
    for n in range(1, groups):
        w_dp(n, grp).start()

    def pass_on(i, zd, buf, sems, to):
        return pltpu.make_async_remote_copy(
            src_ref=acc.at[zd, rows(i)], dst_ref=buf.at[zd, rows(i)], send_sem=acc_s.at[i, zd],
            recv_sem=sems.at[i, zd], device_id={"mp": to}, device_id_type=MESH,
        )

    def both(i, zd):
        return part[2 * zd + c, rows(i)].astype(F32) + sib_buf[zd, rows(i)].astype(F32)

    def arrive(i, zd):
        pair(i, zd).wait_recv()

    def step(i, zd, buf, sems, first, to):
        arrive(i, zd)

        @pl.when(first)
        def _():
            acc[zd, rows(i)] = both(i, zd).astype(BF16)

        @pl.when(jnp.logical_not(first))
        def _():
            pass_on(i, zd, buf, sems, to).wait_recv()
            acc[zd, rows(i)] = (both(i, zd) + buf[zd, rows(i)].astype(F32)).astype(BF16)

        pass_on(i, zd, buf, sems, to).start()

    def sums(i, k):
        rd, ld = chips - 1 - k, k
        when(rd > z, functools.partial(step, i, rd, from_l, fl_r, z == 0, me + 2))
        when(ld < z, functools.partial(step, i, ld, from_r, fr_r, z == chips - 1, me - 2))

    first = [
        Line(chips, lambda j, i=i: att.at[j, rows(i)], g1_r.at[i], g1_a.at[i], g1_b.at[i], g1_c.at[i])
        for i in range(chunks)
    ]
    second = [
        Line(chips, lambda j, i=i: hcol.at[j, i], g2_r.at[i], g2_a.at[i], g2_b.at[i], g2_c.at[i])
        for i in range(chunks)
    ]

    def attended(i):
        arrive(i, z)
        tot[...] = both(i, z)

        @pl.when(z > 0)
        def _():
            pass_on(i, z, from_l, fl_r, me).wait_recv()
            tot[...] += from_l[z, rows(i)].astype(F32)

        @pl.when(z < chips - 1)
        def _():
            pass_on(i, z, from_r, fr_r, me).wait_recv()
            tot[...] += from_r[z, rows(i)].astype(F32)

        for h in range(HEADS):
            cols = slice(h * hd, (h + 1) * hd)
            att[me, rows(i), cols] = (tot[:, cols] / tot[:, width + h : width + h + 1]).astype(BF16)
        first[i].start()

    def project(i):
        first[i].arrive()
        if i == 0:
            load_res.wait()
            for k in range(1, groups):
                w_dp(k, lax.rem(grp + groups - k, groups)).wait_recv()
        projected = jnp.dot(
            att[:, rows(i), :].reshape(shards * CHUNK, width),
            wcol[...].reshape(width, ncol),
            preferred_element_type=F32,
        )
        res = res_ref[:, rows(i), :].reshape(shards * CHUNK, ncol)
        hcol[me, i] = (res.astype(F32) + projected).astype(BF16)
        second[i].start()

    def total_copy(i, n):
        return pltpu.make_async_remote_copy(
            src_ref=stats.at[i], dst_ref=slots.at[n, i], send_sem=t_s.at[i, n],
            recv_sem=t_r.at[i, n], device_id={"mp": lax.rem(me + n, shards)}, device_id_type=MESH,
        )

    def score(i):
        count = shards * CHUNK
        h = out_ref[:, rows(i), :].reshape(count, width).astype(F32)
        normed = (
            h * lax.rsqrt(jnp.mean(h * h, -1, keepdims=True) + 1e-06) * gain_ref[...]
        ).astype(BF16)
        lane = lax.broadcasted_iota(jnp.int32, (count, 128), 1)
        marks = []
        for n, ahead in enumerate((1, 2, 0)):
            low = i * CHUNK + ahead
            marks.append(
                jnp.concatenate(
                    [mark[low : low + CHUNK, 8 * n + t : 8 * n + t + 1] for t in range(shards)], 0
                ).astype(jnp.int32)
            )
        new = [jnp.zeros((count, 128), F32) for _ in range(4)]
        for low in range(0, vocab, 512):
            high = min(low + 512, vocab)
            logits = jnp.dot(normed, vbuf[:, low:high], preferred_element_type=F32)
            for b in range(0, high - low, 128):
                x = logits[:, b : b + 128]
                new[0] += jnp.exp(x)
                for n in range(3):
                    new[n + 1] += jnp.where(lane + (low + b) == marks[n], x, 0.0)
        stat = jnp.zeros((count, 128), F32)
        for n in range(4):
            stat = jnp.where(lane == n, jnp.sum(new[n], -1, keepdims=True), stat)
        stats[i] = jnp.transpose(stat)[:8]
        for n in range(1, shards):
            total_copy(i, n).start()

    def place(i):
        second[i].arrive()
        for j in range(shards):
            for t in range(shards):
                out_ref[t, rows(i), j * ncol : (j + 1) * ncol] = hcol[
                    j, i, t * CHUNK : (t + 1) * CHUNK
                ]

    def finish_hidden(i):
        second[i].forward(chips - 1)
        place(i)

    def finish_scores(i):
        if i == 0:
            load_vocab.wait()
        score(i)

    stages = [lambda i, k=k: sums(i, k) for k in range(chips - 1)]
    stages += [attended]
    stages += [lambda i, k=k: first[i].forward(k) for k in range(1, chips)]
    stages += [project]
    stages += [lambda i, k=k: second[i].forward(k) for k in range(1, chips - 1)]
    stages += [finish_hidden, finish_scores]
    for turn in range(len(stages) + chunks - 1):
        live = [i for i in range(chunks) if 0 <= turn - i < len(stages)]
        for i in sorted(live, key=lambda i: stages[turn - i] is finish_scores):
            stages[turn - i](i)
    for i in range(chunks):
        total = stats[i]
        for n in range(1, shards):
            total_copy(i, n).wait_recv()
            total = total + slots[n, i]
        stat_ref[i] = total

    for i in range(chunks):
        first[i].finish()
        second[i].finish()
        for zd in range(chips):
            pair(i, zd).wait_send()
            when(zd != z, lambda: pass_on(i, zd, from_l, fl_r, me).wait_send())
    for k in range(1, shards):
        w_mp(k).wait_send()
    for k in range(1, groups):
        w_dp(k, grp).wait_send()
    for i in range(chunks):
        for n in range(1, shards):
            total_copy(i, n).wait_send()


def hidden_of(
    shards, groups, lengths, queries, cache_keys, cache_values, new_keys, new_values, parents,
    tree_tokens, residual, out_weight, gain, vocab_weight,
):
    own, width = queries.shape[1:]
    wide = width + 128
    ncol = width // shards
    chips = shards // 2
    chunks = own // CHUNK
    dma = pltpu.SemaphoreType.DMA
    anywhere = pl.BlockSpec(memory_space=pl.ANY)
    gather_sems = [dma((chunks, shards))] + [dma((chunks, chips))] * 3
    vmem = pl.BlockSpec(memory_space=pltpu.VMEM)
    return pl.pallas_call(
        functools.partial(hidden_kernel, chips, groups),
        in_specs=[pl.BlockSpec(memory_space=pltpu.SMEM)] + [anywhere] * 8 + [vmem, vmem, anywhere],
        out_specs=[vmem, vmem],
        out_shape=[
            jax.ShapeDtypeStruct((shards, own, width), BF16),
            jax.ShapeDtypeStruct((chunks, 8, shards * CHUNK), F32),
        ],
        scratch_shapes=[
            pltpu.VMEM(queries.shape, BF16),
            pltpu.VMEM(cache_keys.shape, BF16),
            pltpu.VMEM(cache_values.shape, BF16),
            pltpu.VMEM(new_keys.shape, BF16),
            pltpu.VMEM(new_values.shape, BF16),
            pltpu.VMEM(parents.shape, jnp.int32),
            pltpu.VMEM(tree_tokens.shape, jnp.int32),
            pltpu.VMEM((shards, own, ncol), BF16),
            pltpu.VMEM((own, shards, 128), F32),
            pltpu.VMEM((128, 128), F32),
            pltpu.VMEM((shards, own, wide), BF16),
            dma((shards,)), dma((shards,)), dma((shards,)), dma, dma, dma,
            pltpu.VMEM((chips, own, wide), BF16),
            pltpu.VMEM((chips, own, wide), BF16),
            pltpu.VMEM((chips, own, wide), BF16),
            pltpu.VMEM((chips, own, wide), BF16),
            pltpu.VMEM((CHUNK, wide), F32),
            pltpu.VMEM((shards, own, width), BF16),
            pltpu.VMEM((groups, shards, out_weight.shape[0], ncol), BF16),
            pltpu.VMEM((shards, chunks, shards * CHUNK, ncol), BF16),
            *[dma((chunks, chips))] * 5,
            *gather_sems,
            *gather_sems,
            dma((shards,)), dma((shards,)), dma((groups,)), dma((groups,)), dma,
            pltpu.VMEM(vocab_weight.shape, BF16),
            pltpu.VMEM((chunks, 8, shards * CHUNK), F32),
            pltpu.VMEM((shards, chunks, 8, shards * CHUNK), F32),
            dma((chunks, shards)), dma((chunks, shards)), dma,
        ],
        compiler_params=pltpu.CompilerParams(
            collective_id=0, has_side_effects=True, vmem_limit_bytes=VMEM_LIMIT
        ),
        name="hidden_exchange",
    )(
        lengths, queries, cache_keys, cache_values, new_keys, new_values, parents, tree_tokens,
        residual, out_weight, gain, vocab_weight,
    )


def local_fast(
    queries, new_keys, new_values, cache_keys, cache_values, lengths, parents, tree_tokens,
    residual, out_weight, norm_gain, vocab_weight,
):
    reqs, tree, width = queries.shape
    tokens = reqs * tree
    shards = lax.axis_size("mp")
    groups = lax.axis_size("dp")
    idx = jnp.arange(tree, dtype=jnp.int32)[None, :]
    by_one = (parents == idx - 1) & (idx > 0)
    own = tokens // shards
    hidden, stats = hidden_of(
        shards, groups, lengths, queries, cache_keys, cache_values, new_keys, new_values, parents,
        tree_tokens, residual, out_weight, norm_gain.reshape(1, width), vocab_weight,
    )
    total = stats.reshape(own // CHUNK, 8, shards, CHUNK).transpose(1, 2, 0, 3)
    total = total.reshape(8, reqs, tree)

    def behind(x, n):
        return jnp.pad(x[:, : tree - n], ((0, 0), (n, 0)))

    sums = total[0]
    picked = jnp.where(idx == 0, total[3], jnp.where(by_one, behind(total[1], 1), behind(total[2], 2)))
    norm = jnp.where(idx == 0, sums, jnp.where(by_one, behind(sums, 1), behind(sums, 2)))
    return (hidden.reshape(reqs, tree, width), picked - jnp.log(norm))


def local_plain(
    queries,
    new_keys,
    new_values,
    cache_keys,
    cache_values,
    lengths,
    parents,
    tree_tokens,
    residual,
    out_weight,
    norm_gain,
    vocab_weight,
):
    reqs, tree, width = queries.shape
    slots = cache_keys.shape[1]
    head_dim = width // HEADS
    scale = head_dim ** (-0.5)
    shard = lax.axis_index("mp")
    shards = lax.axis_size("mp")
    tokens = reqs * tree
    window = slots * shards // 2
    positions = shard * slots + jnp.arange(slots, dtype=jnp.int32)
    visible = (positions[None, :] < lengths[:, None]) & (
        (positions[None, :] < SINK) | (positions[None, :] >= lengths[:, None] - window)
    )
    q4 = queries.reshape(reqs, tree, HEADS, head_dim)
    k4 = cache_keys.reshape(reqs, slots, HEADS, head_dim)
    v4 = cache_values.reshape(reqs, slots, HEADS, head_dim)
    cache_e = jnp.where(
        visible[:, None, None, :],
        jnp.exp(jnp.einsum("rihd,rshd->rhis", q4, k4, preferred_element_type=jnp.float32) * scale),
        0.0,
    )
    cache_den = jnp.sum(cache_e, -1)
    cache_num = jnp.einsum(
        "rhis,rshd->rihd", cache_e.astype(jnp.bfloat16), v4, preferred_element_type=jnp.float32
    )
    ancestors = ancestor_mask(parents)
    nk4 = new_keys.reshape(reqs, tree, HEADS, head_dim)
    nv4 = new_values.reshape(reqs, tree, HEADS, head_dim)
    tree_e = jnp.where(
        ancestors[:, None],
        jnp.exp(jnp.einsum("rihd,rjhd->rhij", q4, nk4, preferred_element_type=jnp.float32) * scale),
        0.0,
    )
    tree_den = jnp.sum(tree_e, -1)
    tree_num = jnp.einsum(
        "rhij,rjhd->rihd", tree_e.astype(jnp.bfloat16), nv4, preferred_element_type=jnp.float32
    )
    flat_res = residual.reshape(tokens, width)
    num_all, den_all = lax.psum((cache_num.reshape(tokens, width), cache_den), "mp")
    denom = jnp.transpose(den_all + tree_den, (0, 2, 1))
    numer = num_all.reshape(reqs, tree, HEADS, head_dim) + tree_num
    attended = (numer / denom[..., None]).astype(jnp.bfloat16).reshape(tokens, width)
    projected = jnp.dot(
        attended,
        lax.all_gather(out_weight, ("dp", "mp"), axis=0, tiled=True),
        preferred_element_type=jnp.float32,
    )
    hidden = (flat_res.astype(jnp.float32) + projected).astype(jnp.bfloat16)
    hfloat = hidden.astype(jnp.float32)
    normed = (
        hfloat * lax.rsqrt(jnp.mean(hfloat * hfloat, -1, keepdims=True) + 1e-06) * norm_gain
    ).astype(jnp.bfloat16)
    vocab_dev = vocab_weight.shape[1]
    logits = jnp.dot(normed, vocab_weight, preferred_element_type=jnp.float32)
    exp_sums = jnp.sum(jnp.exp(logits), -1)
    parent_rows = (jnp.arange(reqs, dtype=jnp.int32)[:, None] * tree + parents).reshape(-1)
    column = tree_tokens.reshape(-1) - shard * vocab_dev
    inside = (column >= 0) & (column < vocab_dev)
    picked = jnp.where(inside, logits[parent_rows, jnp.clip(column, 0, vocab_dev - 1)], 0.0)
    parent_sums = exp_sums[parent_rows]
    total_sums, total_picked = lax.psum((parent_sums, picked), "mp")
    node_logprob = (total_picked - jnp.log(total_sums)).reshape(reqs, tree)
    return (hidden.reshape(reqs, tree, width), node_logprob)


def local(*args):
    queries, vocab_weight = args[0], args[-1]
    reqs, tree, width = queries.shape
    shards = lax.axis_size("mp")
    fits = (
        (reqs * tree) % (shards * 16) == 0
        and width % (shards * 128) == 0
        and width == HEADS * 128
        and tree % 16 == 0
        and vocab_weight.shape[1] % 128 == 0
        and shards % 2 == 0
        and shards == 8
        and reqs == shards
    )
    return (local_fast if fits else local_plain)(*args)


def solution(mesh):
    placed = (
        P("dp", None, None),
        P("dp", None, None),
        P("dp", None, None),
        P("dp", "mp", None),
        P("dp", "mp", None),
        P("dp"),
        P("dp", None),
        P("dp", None),
        P("dp", None, None),
        P(("dp", "mp"), None),
        P(),
        P(None, "mp"),
    )
    return jax.shard_map(
        local,
        mesh=mesh,
        in_specs=placed,
        out_specs=(P("dp", None, None), P("dp", None)),
        check_vma=False,
    )
```
